512 devices in a mesh: req: 32 (over z, core), exp: 16 (over y, x).
Axes of the slice: x: 4, y: 4, z: 16, core: 2. Of those that a mesh axis runs over, the one named last changes fastest.
Arguments:
- queries: bfloat16 [256, 8192], P('req'), may hold values from -80 to 80
- new_keys: bfloat16 [256, 512], P('req'), may hold values from -12 to 12
- new_values: bfloat16 [256, 512], P('req'), may hold values from -18 to 18
- key_cache: bfloat16 [64, 384, 16, 512], P('req', None, 'exp'), may hold values from -12 to 12
- value_cache: bfloat16 [64, 384, 16, 512], P('req', None, 'exp'), may hold values from -18 to 18
- lengths: int32 [64], replicated, may hold values from 1 to 6144, as said below
- out_proj: bfloat16 [8192, 4096], P('exp', 'req'), may hold values from -0.0625 to 0.0625
- residual: bfloat16 [256, 4096], P(None, 'req'), may hold values from -6 to 6
- norm_gain: float32 [4096], P('req'), may hold values from 0.5 to 1.5
- gate_weight: bfloat16 [32, 4096, 1536], P('exp', 'req'), may hold values from -0.09375 to 0.09375
- up_weight: bfloat16 [32, 4096, 1536], P('exp', 'req'), may hold values from -0.09375 to 0.09375
- down_weight: bfloat16 [32, 1536, 4096], P('exp', None, 'req'), may hold values from -0.15625 to 0.15625
- expert_ids: int32 [256, 8], replicated, may hold values from 0 to 31, all different within a row; in each aligned block of 256 rows (0 to 255, 256 to 511, ...) at most 128 rows name the same one
- route_weights: float32 [256, 8], replicated, may hold values from 0.1 to 1
Outputs:
- layer_out: bfloat16 [256, 4096], P('exp', 'req')
The draws below stay inside these ranges and needn't reach their ends.
Inputs may be any that keep to these rules, and one draw needn't show every extreme that they name: `lengths`: some request has exactly 6144 cached tokens. `expert_ids`: each row names 8 different experts; no expert is named by more than 128 rows, a bound that some block reaches.
All inputs are finite; a program needn't handle non-finite values.
Results may differ from the reference program's by a relative error of at most 0.014.
Values may be sent and summed in bfloat16 or wider, within the bound.
A program may use at most 64 MiB of HBM per device.

```python
import math
import jax
import jax.numpy as jnp
import numpy as np
from jax import lax

D = 4096
QH = 64
KVH = 4
HD = 128
FF = 1536
TOP = 8
STEPS = 4
CAP_DEV = 384
EXPERTS = 32
CAP = 6144
REQS = 64
TOKENS = 256
ROUTE_CAP = 128
N_EXP = 16


def draw_queries(key, part):
    key = jax.random.fold_in(key, 11)
    values = jnp.clip(jax.random.normal(key, (TOKENS, QH * HD), jnp.float32), -6.0, 6.0)
    return values.astype(jnp.bfloat16)


def draw_lengths(key, part):
    key = jax.random.fold_in(key, 5)
    short_len = jax.random.randint(jax.random.fold_in(key, 1), (REQS,), 1, CAP // 4 + 1)
    order_ids = jax.random.permutation(jax.random.fold_in(key, 2), REQS)
    return jnp.where(order_ids < max(1, REQS // 16), CAP, short_len).astype(jnp.int32)


def steps_of(key, extent, pieces, low, largest):
    level = 1.0
    for dim, shards_of in pieces:
        steps = jax.random.uniform(jax.random.fold_in(jax.random.fold_in(key, 6), dim), (shards_of,), jnp.float32, low / len(pieces), largest / len(pieces))
        level = level * jnp.repeat(jnp.exp(steps), extent[dim] // shards_of).reshape((-1,) + (1,) * (len(extent) - 1 - dim))
    return level


def deal_out(stream_key, own, number, rows, number_of, top, reach, lean):
    order = jax.random.permutation(stream_key, number_of)
    heavy_load, usual = portions_of(number_of, rows * top, reach, lean, True), portions_of(number_of, rows * top, reach, lean, False)
    places = jnp.arange(number_of)

    def named(sizes, turn):
        used = int((sizes > 0).sum())
        fixed = max(1, used // 4)
        passed = fixed + (places - fixed + turn * (used - fixed)) % max(1, number_of - fixed)
        return jnp.zeros((number_of,), jnp.int32).at[order[jnp.where(places < fixed, places, passed)]].set(jnp.asarray(sizes, jnp.int32))

    sizes = jnp.where(number % 4 == 0, named(heavy_load, number // 4), named(usual, number - number // 4 - 1))
    mixed = jax.random.permutation(jax.random.fold_in(own, 3), number_of)
    giver, taker = mixed[0:number_of // 2 * 2:2], mixed[1:number_of // 2 * 2:2]
    room = jnp.minimum(sizes[giver] - 1, reach - sizes[taker]) // 2
    room = jnp.where((giver == order[0]) | (taker == order[0]) | (sizes[taker] == 0), 0, jnp.maximum(room, 0))
    passed = jax.random.randint(jax.random.fold_in(own, 4), (number_of // 2,), 0, 1 << 20) % (room + 1)
    sizes = sizes.at[giver].add(-passed).at[taker].add(passed)
    labels = jnp.searchsorted(jnp.cumsum(sizes), jnp.arange(rows * top), side="right").astype(jnp.int32)
    table = labels.reshape(top, rows).T
    table = table[jax.random.permutation(jax.random.fold_in(own, 1), rows)]
    turn = jax.random.randint(jax.random.fold_in(own, 2), (rows, 1), 0, top)
    return jnp.take_along_axis(table, (jnp.arange(top)[None, :] + turn) % top, axis=1)


def portions_of(amount, total, most, slope, full):
    loads = [(1 << 20) // math.isqrt(standing ** slope) + 1 for standing in range(1, amount + 1)]
    largest = most if full else min(most, max(-(-total // amount), total * loads[0] // sum(loads)))
    least = 1 if total - largest >= amount - 1 else 0
    given, surplus = [largest] + [least] * (amount - 1), total - largest - least * (amount - 1)
    while surplus > 0:
        movable = [i for i in range(1, amount) if given[i] < largest] or [i for i in range(1, amount) if given[i] < most]
        mass, remaining = sum([loads[i] for i in movable]), surplus
        for i in movable:
            addition = min(most - given[i], max(1, remaining * loads[i] // mass), surplus)
            given[i] = given[i] + addition
            surplus = surplus - addition
    return np.array(given)


def bell_draw(rng, shape, width, bound, shards=(), kind=jnp.bfloat16):
    gain = steps_of(rng, shape, shards, -0.22, 0.18) if shards else 1.0
    array = jax.random.normal(rng, shape, jnp.float32) * width * gain
    return jnp.minimum(jnp.maximum(array, -bound), bound).astype(kind)


def setup_inputs(seed: int = 0) -> dict:
    key_of = jax.random.split(jax.random.key(seed), 15)
    queries = draw_queries(jax.random.fold_in(key_of[14], 71), 0)
    new_keys = bell_draw(key_of[1], (TOKENS, KVH * HD), 2.0, 12.0, ((0, 32),))
    new_values = bell_draw(key_of[2], (TOKENS, KVH * HD), 3.0, 18.0, ((0, 32),))
    key_cache = bell_draw(key_of[3], (REQS, CAP_DEV, N_EXP, KVH * HD), 2.0, 12.0, ((0, 32), (2, 16)))
    value_cache = bell_draw(key_of[4], (REQS, CAP_DEV, N_EXP, KVH * HD), 3.0, 18.0, ((0, 32), (2, 16)))
    lengths = draw_lengths(jax.random.fold_in(key_of[14], 71), 0)
    out_proj = bell_draw(key_of[6], (QH * HD, D), (QH * HD) ** -0.5, 0.0625, ((0, 16), (1, 32)))
    residual = bell_draw(key_of[7], (TOKENS, D), 1.0, 6.0, ((1, 32),))
    norm_gain = jnp.clip(1.0 + 0.1 * jax.random.normal(key_of[8], (D,), jnp.float32), 0.5, 1.5)
    gate_weight = bell_draw(key_of[9], (EXPERTS, D, FF), D ** -0.5, 0.09375, ((0, 16), (1, 32)))
    up_weight = bell_draw(key_of[10], (EXPERTS, D, FF), D ** -0.5, 0.09375, ((0, 16), (1, 32)))
    down_weight = bell_draw(key_of[11], (EXPERTS, FF, D), FF ** -0.5, 0.15625, ((0, 16), (2, 32)))
    expert_ids_keys = jax.random.split(jax.random.fold_in(key_of[12], 1), TOKENS // TOKENS)
    expert_ids_turns = jax.random.permutation(jax.random.fold_in(key_of[12], 3), TOKENS // TOKENS)
    expert_ids = jax.vmap(lambda own, number: deal_out(jax.random.fold_in(key_of[12], 2), own, number, TOKENS, EXPERTS, TOP, ROUTE_CAP, 1))(expert_ids_keys, expert_ids_turns).reshape((TOKENS, TOP))
    route_weights = jnp.clip(jax.random.uniform(key_of[13], (TOKENS, TOP), jnp.float32, 0.1, 1.0), 0.1, 1.0)
    return {"queries": queries, "new_keys": new_keys, "new_values": new_values, "key_cache": key_cache, "value_cache": value_cache, "lengths": lengths, "out_proj": out_proj, "residual": residual, "norm_gain": norm_gain, "gate_weight": gate_weight, "up_weight": up_weight, "down_weight": down_weight, "expert_ids": expert_ids, "route_weights": route_weights}


def attend(operands):
    query_rows, fresh_keys, fresh_values, cache_keys, cache_values, length = operands
    group_n = QH // KVH
    query_grid = query_rows.astype(jnp.float32).reshape(STEPS, KVH, group_n, HD)
    all_keys = jnp.concatenate([cache_keys, fresh_keys], axis=0).astype(jnp.float32).reshape(CAP + STEPS, KVH, HD)
    all_values = jnp.concatenate([cache_values, fresh_values], axis=0).astype(jnp.float32).reshape(CAP + STEPS, KVH, HD)
    scores = jnp.einsum('tgjd,kgd->gtjk', query_grid, all_keys) * HD ** (-0.5)
    position = jnp.arange(CAP + STEPS, dtype=jnp.int32)
    step_ids = jnp.arange(STEPS, dtype=jnp.int32)
    visible = jnp.where(position[None, :] < CAP, position[None, :] < length, position[None, :] - CAP <= step_ids[:, None])
    scores = jnp.where(visible[None, :, None, :], scores, -jnp.inf)
    row_max = lax.optimization_barrier(jnp.max(scores, axis=-1, keepdims=True))
    weights = jnp.exp(scores - row_max)
    totals = lax.optimization_barrier(jnp.sum(weights, axis=-1))
    rounded = lax.optimization_barrier(weights.astype(jnp.bfloat16)).astype(jnp.float32)
    mixed = jnp.einsum('gtjk,kgd->tgjd', rounded, all_values) / jnp.transpose(totals, (1, 0, 2))[..., None]
    return mixed.reshape(STEPS, QH * HD).astype(jnp.bfloat16)

def reference(queries, new_keys, new_values, key_cache, value_cache, lengths, out_proj, residual, norm_gain, gate_weight, up_weight, down_weight, expert_ids, route_weights):
    kv_width = KVH * HD
    attention = lax.map(attend, (queries.reshape(REQS, STEPS, QH * HD), new_keys.reshape(REQS, STEPS, kv_width), new_values.reshape(REQS, STEPS, kv_width), key_cache.reshape(REQS, CAP, kv_width), value_cache.reshape(REQS, CAP, kv_width), lengths))
    attention = attention.reshape(TOKENS, QH * HD)
    projected = jnp.dot(attention, out_proj, preferred_element_type=jnp.float32)
    hidden_state = residual.astype(jnp.float32) + projected
    norm_scale = lax.rsqrt(lax.optimization_barrier(jnp.mean(hidden_state * hidden_state, axis=1)) + 1e-06)[:, None]
    normed = (hidden_state * norm_gain).astype(jnp.bfloat16)

    def expert_step(running, operands):
        w_gate, w_up, w_down, expert_id = operands
        gate_proj = norm_scale * jnp.dot(normed, w_gate, preferred_element_type=jnp.float32)
        upward = norm_scale * jnp.dot(normed, w_up, preferred_element_type=jnp.float32)
        activated = (jax.nn.silu(gate_proj) * upward).astype(jnp.bfloat16)
        weight_row = lax.optimization_barrier(jnp.sum(jnp.where(expert_ids == expert_id, route_weights, 0.0), axis=1))
        return (running + weight_row[:, None] * jnp.dot(activated, w_down, preferred_element_type=jnp.float32), None)
    moe_sum, _ = lax.scan(expert_step, jnp.zeros((TOKENS, D), jnp.float32), (gate_weight, up_weight, down_weight, jnp.arange(EXPERTS, dtype=jnp.int32)))
    return (hidden_state + moe_sum).astype(jnp.bfloat16)
```

```python
import functools

import jax
import jax.numpy as jnp
from jax import lax
from jax.experimental import pallas as pl
from jax.experimental.pallas import tpu as pltpu
from jax.sharding import PartitionSpec as P

MESH = pl.DeviceIdType.MESH
BF = jnp.bfloat16
F32 = jnp.float32

D = 4096
HD = 128
GROUPS = 4
NZ = 16
NE = 16
SLOTS = 256
TOKENS = 256
HALF = 768
WIDE = 2 * HALF + 128
NEG = -1e30
EPS = 1e-6
CENTERS = (-6, -3, 0, 3, 6)
FAR = (6, -6, 3, -3)


def remote(src, dst, send, recv, dev):
    return pltpu.make_async_remote_copy(
        src_ref=src, dst_ref=dst, send_sem=send, recv_sem=recv, device_id=dev, device_id_type=MESH
    )


def dot(a, b):
    return jnp.dot(a, b, preferred_element_type=F32)


def dot_t(a, b):
    return lax.dot_general(a, b, (((0,), (0,)), ((), ())), preferred_element_type=F32)


def dot_nt(a, b):
    return lax.dot_general(a, b, (((1,), (1,)), ((), ())), preferred_element_type=F32)


def hi_lo(v, rows):
    high = v.astype(BF).astype(F32)
    lane = lax.broadcasted_iota(jnp.int32, (rows, 128), 1)
    return jnp.where(lane < 64, high, v - high).astype(BF)


def from_hi_lo(block):
    return jnp.sum(block, axis=1, keepdims=True) * (1.0 / 64.0)


def kernel(
    len_ref, q_ref, nk_ref, nv_ref, kc_ref, vc_ref, op_ref, res_ref, gain_ref, gw_ref, uw_ref, dw_ref,
    ids_ref, rw_ref, o_ref,
    kc, vc, opw, resb, gainb, wg, wu, wd, resf,
    acc, stat, acc_in, stat_in, wt, attn, cs1, cr1, cs2, cr2,
    nb, hb, sel_in, sel_out, slot_w, part, from_left, from_right, from_far, s2, r2, own, act, mo, fr,
    loc, snd, rcv, bulk_s, bulk_r,
):
    r = lax.axis_index("req")
    e = lax.axis_index("exp")
    z = r // 2
    c = lax.rem(r, 2)
    oc = 1 - c
    ex = lax.rem(e, 4)
    ey = e // 4

    def at_z(off):
        return (2 * lax.rem(z + off + NZ, NZ) + c, e)

    sibling = (2 * z + oc, e)

    barrier = pltpu.get_barrier_semaphore()

    def greet(dev):
        pl.semaphore_signal(barrier, inc=1, device_id=dev, device_id_type=MESH)

    for off in (6, -6, 3, -3, 2, -2, 1, -1):
        greet(at_z(off))

    def greet_plane(i, carry):
        other = lax.rem(e + i, NE)
        greet((r, other))
        greet((2 * z + oc, other))
        return carry

    lax.fori_loop(1, NE, greet_plane, 0)
    greet(sibling)

    copies = []

    def fetch(src, dst):
        cp = pltpu.make_async_copy(src, dst, loc.at[len(copies)])
        cp.start()
        copies.append(cp)
        return cp

    cache_copies = []
    for s in range(2):
        cache_copies.append(fetch(kc_ref.at[s], kc.at[s]))
        cache_copies.append(fetch(vc_ref.at[s], vc.at[s]))
    mine = pl.multiple_of(c * HALF, 128)
    theirs = pl.multiple_of(oc * HALF, 128)
    early = [fetch(op_ref, opw.at[c]), fetch(res_ref, resb.at[c])]
    weights = [
        fetch(gw_ref.at[:, :, pl.ds(mine, HALF)], wg.at[:, c]),
        fetch(uw_ref.at[:, :, pl.ds(mine, HALF)], wu.at[:, c]),
        fetch(dw_ref.at[:, pl.ds(mine, HALF), :], wd.at[:, c]),
    ]
    gainb[c] = jnp.broadcast_to(gain_ref[...], (8, 128))

    lane = lax.broadcasted_iota(jnp.int32, (1, 128), 1)
    lane_slot = lax.rem(lane, 8) // 4
    lane_step = lax.rem(lane, 4)
    first = lane_slot == 0
    n0 = len_ref[2 * r]
    n1 = len_ref[2 * r + 1]
    count = jnp.where(first, n0, n1)
    place = lax.broadcasted_iota(jnp.int32, (384, 128), 0) * NE + e
    live = place < count
    fresh_row = lax.broadcasted_iota(jnp.int32, (16, 128), 0)
    fresh_live = (
        (fresh_row < 8)
        & (fresh_row // 4 == lane_slot)
        & (lax.rem(fresh_row, 4) <= lane_step)
        & (jnp.zeros((16, 128), jnp.int32) + e == 0)
    )
    zeros8 = jnp.zeros((8, 512), F32)
    fresh_k = jnp.concatenate([nk_ref[...].astype(F32), zeros8], axis=0).astype(BF)
    fresh_v = jnp.concatenate([nv_ref[...].astype(F32), zeros8], axis=0).astype(BF)
    scale = HD ** (-0.5)
    for cp in cache_copies:
        cp.wait()
    stat_row = lax.broadcasted_iota(jnp.int32, (8, 128), 0)
    for g in range(GROUPS):
        cols = slice(g * HD, (g + 1) * HD)
        q = jnp.concatenate(
            [q_ref[:, (g * 16 + j) * HD:(g * 16 + j + 1) * HD].astype(F32) for j in range(16)], axis=0
        ).astype(BF)
        s0 = dot_nt(kc[0, :, cols], q)
        s1 = dot_nt(kc[1, :, cols], q)
        score = jnp.where(live, jnp.where(first, s0, s1) * scale, NEG)
        fresh = jnp.where(fresh_live, dot_nt(fresh_k[:, cols], q) * scale, NEG)
        top = jnp.maximum(jnp.max(score, axis=0, keepdims=True), jnp.max(fresh, axis=0, keepdims=True))
        w = jnp.where(live, jnp.exp(score - top), 0.0)
        wf = jnp.where(fresh_live, jnp.exp(fresh - top), 0.0)
        total = jnp.sum(w, axis=0, keepdims=True) + jnp.sum(wf, axis=0, keepdims=True)
        w0 = jnp.where(first, w, 0.0).astype(BF)
        w1 = jnp.where(first, 0.0, w).astype(BF)
        mixed = dot_t(w0, vc[0, :, cols]) + dot_t(w1, vc[1, :, cols]) + dot_t(wf.astype(BF), fresh_v[:, cols])
        acc[g] = mixed.astype(BF)
        stat[g] = jnp.where(stat_row == 0, top, total)

    for cp in early:
        cp.wait()
    pl.semaphore_wait(barrier, 8 + 2 * (NE - 1) + 1)

    def acc_copy(i):
        other = lax.rem(e + i, NE)
        rows = pl.ds(pl.multiple_of(32 * lax.rem(other, 4), 32), 32)
        return (
            remote(acc.at[other // 4, rows], acc_in.at[e], bulk_s.at[0], bulk_r.at[0], (r, other)),
            remote(stat.at[other // 4], stat_in.at[e], bulk_s.at[1], bulk_r.at[1], (r, other)),
        )

    def acc_send(i, carry):
        for cp in acc_copy(i):
            cp.start()
        return carry

    lax.fori_loop(1, NE, acc_send, 0)

    sends = []

    def send(src, dst, dev):
        cp = remote(src, dst, snd.at[len(sends)], rcv.at[len(sends)], dev)
        cp.start()
        sends.append(cp)
        return cp

    opw_cp = send(op_ref, opw.at[c], sibling)
    res_cp = send(res_ref, resb.at[c], sibling)
    gain_cp = send(gainb.at[c], gainb.at[c], sibling)
    wg_cp = send(gw_ref.at[:, :, pl.ds(theirs, HALF)], wg.at[:, c], sibling)
    wu_cp = send(uw_ref.at[:, :, pl.ds(theirs, HALF)], wu.at[:, c], sibling)
    wd_cp = send(dw_ref.at[:, pl.ds(theirs, HALF), :], wd.at[:, c], sibling)

    acc_in[e] = acc[ey, pl.ds(pl.multiple_of(32 * ex, 32), 32)]
    stat_in[e] = stat[ey]

    ids = ids_ref[...]
    rw = rw_ref[...]
    col = lax.broadcasted_iota(jnp.int32, (256, 256), 1)
    row = lax.broadcasted_iota(jnp.int32, (256, 256), 0)
    upto = jnp.where(row <= col, 1.0, 0.0).astype(BF)
    real = (lax.rem(col, 128) // 8) * 16 + (col // 128) * 8 + lax.rem(col, 8)
    perm = jnp.where(row == real, 1.0, 0.0).astype(BF)
    row8 = lax.broadcasted_iota(jnp.int32, (8, 256), 0)
    hit0 = ids == 2 * e
    hit1 = ids == 2 * e + 1
    on0 = jnp.max(jnp.where(hit0, 1.0, 0.0), axis=0, keepdims=True)
    on1 = jnp.max(jnp.where(hit1, 1.0, 0.0), axis=0, keepdims=True)
    rw0 = jnp.sum(jnp.where(hit0, rw, 0.0), axis=0, keepdims=True)
    rw1 = jnp.sum(jnp.where(hit1, rw, 0.0), axis=0, keepdims=True)
    on = jnp.where(row8 == 0, on0, jnp.where(row8 == 1, on1, 0.0))
    rank = dot(on.astype(BF), upto)
    pos = jnp.where(on > 0.5, rank, 0.0)
    pos_perm = dot(pos.astype(BF), perm)
    slot_id = lax.broadcasted_iota(jnp.int32, (128, 256), 0).astype(F32) + 1.0
    chosen = []
    for k, weight in ((0, rw0), (1, rw1)):
        here = pl.ds(128 * k, 128)
        sel_in[here, :] = jnp.where(pos_perm[k:k + 1, :] == slot_id, 1.0, 0.0).astype(BF)
        pick = jnp.where(pos[k:k + 1, :] == slot_id, 1.0, 0.0)
        slot_w[here, :] = jnp.broadcast_to(jnp.sum(pick * weight, axis=1, keepdims=True), (128, 128))
        chosen.append(pick)
    sel_out[...] = jnp.transpose(jnp.concatenate(chosen, axis=0)).astype(BF)

    pltpu.make_async_copy(acc_in.at[pl.ds(0, NE - 1)], acc_in.at[pl.ds(0, NE - 1)], bulk_r.at[0]).wait()
    pltpu.make_async_copy(stat_in.at[pl.ds(0, NE - 1)], stat_in.at[pl.ds(0, NE - 1)], bulk_r.at[1]).wait()
    tops = stat_in[:, 0, :]
    totals = stat_in[:, 1, :]
    rel = jnp.exp(tops - jnp.max(tops, axis=0, keepdims=True))
    rel = rel / jnp.sum(rel * totals, axis=0, keepdims=True)
    wt[...] = jnp.transpose(jnp.concatenate([rel, jnp.zeros((112, 128), F32)], axis=0))
    shares = wt[pl.ds(pl.multiple_of(32 * ex, 32), 32), :]
    merged = shares[:, 0:1] * acc_in[0].astype(F32)
    for src in range(1, NE):
        merged = merged + shares[:, src:src + 1] * acc_in[src].astype(F32)
    attn[z] = merged.astype(BF)

    def gather(chunk):
        first_leg = {off: send(chunk(z), chunk(z), at_z(off)) for off in FAR}
        last_leg = [send(chunk(z), chunk(z), at_z(off)) for off in (1, -1)]
        for off in (3, -3, 6, -6):
            first_leg[off].wait_recv()
            src = lax.rem(z - off + NZ, NZ)
            for step in (1, -1):
                last_leg.append(send(chunk(src), chunk(src), at_z(step)))
        way = 1 - 2 * c
        src = lax.rem(z - 6 * way + NZ, NZ)
        last_leg.append(send(chunk(src), chunk(src), at_z(2 * way)))
        for cp in last_leg:
            cp.wait_recv()

    gather(lambda i: attn.at[i])

    opw_cp.wait_recv()
    res_cp.wait_recv()
    gain_cp.wait_recv()
    for k in range(2):
        blocks = resb[k].astype(F32).reshape(NZ, 2, 8, 128)
        resf[k] = jnp.where(c == 0, blocks[:, 0], blocks[:, 1]).reshape(128, 128)
    heads = attn[...].astype(F32).reshape(NZ, 4, 8, 128)
    x = jnp.concatenate([heads[:, j].reshape(128, 128) for j in range(4)], axis=1).astype(BF)

    def row_peer(k):
        return (r, ey * 4 + lax.rem(ex + k, 4))

    def column_peer(k):
        return (r, lax.rem(ey + k, 4) * 4 + ex)

    first_sum = []
    proj = []
    for k, peer in ((0, row_peer), (1, column_peer)):
        proj.append(dot(x, opw[k]))
        cs1[k] = proj[k].astype(BF)
        first_sum.append([send(cs1.at[k], cr1.at[k, i - 1], peer(i)) for i in (2, 1, 3)])
    second_sum = []
    for k, peer in ((0, column_peer), (1, row_peer)):
        for cp in first_sum[k]:
            cp.wait_recv()
        for i in range(3):
            proj[k] = proj[k] + cr1[k, i].astype(F32)
        cs2[k] = proj[k].astype(BF)
        second_sum.append([send(cs2.at[k], cr2.at[k, i - 1], peer(i)) for i in (2, 1, 3)])
    hidden = []
    square = jnp.zeros((128, 128), F32)
    mine_rows = pl.ds(pl.multiple_of(128 * c, 128), 128)
    for k in range(2):
        for cp in second_sum[k]:
            cp.wait_recv()
        h = proj[k] + resf[k]
        for i in range(3):
            h = h + cr2[k, i].astype(F32)
        hidden.append(h)
        square = square + h * h
        nb[mine_rows, 128 * k:128 * k + 128] = (h * gainb[k, 0:1, :]).astype(BF)
    nb[mine_rows, 256:384] = hi_lo(jnp.sum(square, axis=1, keepdims=True), 128)
    nb_cp = send(nb.at[mine_rows], nb.at[mine_rows], sibling)
    hb[c] = jnp.where(c == 0, hidden[0], hidden[1])
    hb[2] = jnp.where(c == 0, hidden[1], hidden[0])
    hb_cp = send(hb.at[2], hb.at[c], sibling)

    for cp in weights:
        cp.wait()
    wg_cp.wait_recv()
    wu_cp.wait_recv()
    nb_cp.wait_recv()
    rows_in = dot(sel_in[...], nb[...])
    part[:, 2 * HALF:] = hi_lo(from_hi_lo(rows_in[:, 256:384]), SLOTS)
    rows_in = rows_in[:, :256].astype(BF)
    for k in range(2):
        here = slice(128 * k, 128 * k + 128)
        part[here, 0:HALF] = dot(rows_in[here], wg[k].reshape(256, HALF)).astype(BF)
        part[here, HALF:2 * HALF] = dot(rows_in[here], wu[k].reshape(256, HALF)).astype(BF)

    def rows_of(i):
        return pl.ds(pl.multiple_of(16 * lax.rem(i + 2 * NZ, NZ), 16), 16)

    way = 1 - 2 * c
    far_cp = send(part.at[rows_of(z + 8)], from_far, at_z(-2 * way))
    left_cp = [None] * 5
    right_cp = [None] * 5
    for k in (0, 4, 1, 3, 2):
        left_cp[k] = send(part.at[rows_of(z + 1 - CENTERS[k])], from_left.at[k], at_z(1))
        right_cp[k] = send(part.at[rows_of(z - 1 - CENTERS[k])], from_right.at[k], at_z(-1))
    far_cp.wait_recv()
    second = [None] * 5
    for k in (0, 4, 1, 3, 2):
        left_cp[k].wait_recv()
        right_cp[k].wait_recv()
        s = part[rows_of(z - CENTERS[k]), :].astype(F32) + from_left[k].astype(F32) + from_right[k].astype(F32)
        if k == 0:
            s = s + jnp.where(c == 1, from_far[...].astype(F32), 0.0)
        if k == 4:
            s = s + jnp.where(c == 0, from_far[...].astype(F32), 0.0)
        if k == 2:
            own[...] = s
        else:
            s2[k, :, 0:2 * HALF] = s[:, 0:2 * HALF].astype(BF)
            s2[k, :, 2 * HALF:] = hi_lo(from_hi_lo(s[:, 2 * HALF:]), 16)
            second[k] = send(s2.at[k], r2.at[k], at_z(-CENTERS[k]))
    s = own[...]
    for k in (1, 3, 0, 4):
        second[k].wait_recv()
        s = s + r2[k].astype(F32)
    norm = lax.rsqrt(from_hi_lo(s[:, 2 * HALF:]) * (1.0 / D) + EPS)
    gate = norm * s[:, 0:HALF]
    up = norm * s[:, HALF:2 * HALF]
    act[rows_of(z), :] = (gate / (1.0 + jnp.exp(-gate)) * up).astype(BF)

    gather(lambda i: act.at[pl.ds(pl.multiple_of(16 * i, 16), 16)])

    wd_cp.wait_recv()
    for k in range(2):
        down = jnp.concatenate([dot(act[128 * x2:128 * x2 + 128, :], wd[x2, k]) for x2 in range(2)], axis=0)
        mo[k] = dot(sel_out[...], (down * slot_w[...]).astype(BF)).astype(BF)

    def rows_for(other):
        return pl.ds(pl.multiple_of(16 * other, 16), 16)

    def out_copy(i, core):
        other = lax.rem(e + i, NE)
        return remote(
            mo.at[core, rows_for(other)], fr.at[2 * e + c], bulk_s.at[2], bulk_r.at[2], (2 * z + core, other)
        )

    def out_send(i, carry):
        out_copy(i, c).start()
        out_copy(i, oc).start()
        return carry

    lax.fori_loop(1, NE, out_send, 0)
    out_copy(0, oc).start()
    fr[2 * e + c] = mo[c, rows_for(e)]
    hb_cp.wait_recv()
    first_rows = pl.ds(pl.multiple_of(8 * e, 8), 8)
    base = jnp.concatenate([hb[0, first_rows], hb[1, first_rows]], axis=0)
    pltpu.make_async_copy(fr.at[pl.ds(0, 2 * NE - 1)], fr.at[pl.ds(0, 2 * NE - 1)], bulk_r.at[2]).wait()
    o_ref[...] = (base + jnp.sum(fr[...].astype(F32), axis=0)).astype(BF)

    for cp in sends:
        cp.wait_send()
    pltpu.make_async_copy(acc_in.at[pl.ds(0, NE - 1)], acc_in.at[pl.ds(0, NE - 1)], bulk_s.at[0]).wait()
    pltpu.make_async_copy(stat_in.at[pl.ds(0, NE - 1)], stat_in.at[pl.ds(0, NE - 1)], bulk_s.at[1]).wait()
    pltpu.make_async_copy(fr.at[pl.ds(0, 2 * NE - 1)], fr.at[pl.ds(0, 2 * NE - 1)], bulk_s.at[2]).wait()


def layer(
    queries, new_keys, new_values, key_cache, value_cache, lengths, out_proj, residual, norm_gain,
    gate_weight, up_weight, down_weight, expert_ids, route_weights,
):
    vmem = pl.BlockSpec(memory_space=pltpu.VMEM)
    hbm = pl.BlockSpec(memory_space=pl.ANY)
    smem = pl.BlockSpec(memory_space=pltpu.SMEM)
    scratch = [
        ((2, 384, 512), BF), ((2, 384, 512), BF), ((2, 512, 128), BF), ((2, 256, 128), BF), ((2, 8, 128), F32),
        ((2, 2, 128, HALF), BF), ((2, 2, 128, HALF), BF), ((2, 2, HALF, 128), BF), ((2, 128, 128), F32),
        ((4, 128, 128), BF), ((4, 8, 128), F32), ((16, 32, 128), BF), ((16, 8, 128), F32), ((128, 128), F32),
        ((16, 32, 128), BF), ((2, 128, 128), BF), ((2, 3, 128, 128), BF), ((2, 128, 128), BF), ((2, 3, 128, 128), BF),
        ((256, 384), BF), ((3, 128, 128), F32), ((256, 256), BF), ((256, 256), BF), ((256, 128), F32),
        ((256, WIDE), BF), ((5, 16, WIDE), BF), ((5, 16, WIDE), BF), ((16, WIDE), BF),
        ((5, 16, WIDE), BF), ((5, 16, WIDE), BF), ((16, WIDE), F32), ((256, HALF), BF),
        ((2, 256, 128), BF), ((32, 16, 128), BF),
    ]
    sems = [16, 80, 80, 3, 3]
    return pl.pallas_call(
        kernel,
        name="layer",
        out_shape=jax.ShapeDtypeStruct((16, 128), BF),
        in_specs=[smem, vmem, vmem, vmem, hbm, hbm, hbm, hbm, vmem, hbm, hbm, hbm, vmem, vmem],
        out_specs=vmem,
        scratch_shapes=[pltpu.VMEM(s, t) for s, t in scratch] + [pltpu.SemaphoreType.DMA((n,)) for n in sems],
        compiler_params=pltpu.CompilerParams(
            collective_id=0, has_side_effects=True, vmem_limit_bytes=48 * 1024 * 1024
        ),
    )(
        lengths, queries, new_keys, new_values, key_cache[:, :, 0, :], value_cache[:, :, 0, :], out_proj, residual,
        norm_gain.reshape(1, 128), gate_weight, up_weight, down_weight, expert_ids.T, route_weights.T,
    )


def solution(mesh):
    in_specs = (
        P("req", None), P("req", None), P("req", None), P("req", None, "exp", None), P("req", None, "exp", None),
        P(), P("exp", "req"), P(None, "req"), P("req"), P("exp", "req", None), P("exp", "req", None),
        P("exp", None, "req"), P(), P(),
    )
    return jax.shard_map(layer, mesh=mesh, in_specs=in_specs, out_specs=P("exp", "req"), check_vma=False)
```

```python
import functools

import jax
import jax.numpy as jnp
from jax import lax
from jax.experimental import pallas as pl
from jax.experimental.pallas import tpu as pltpu
from jax.sharding import PartitionSpec as P

MESH = pl.DeviceIdType.MESH
BF = jnp.bfloat16
F32 = jnp.float32

D = 4096
HD = 128
GROUPS = 4
NZ = 16
NE = 16
SLOTS = 256
TOKENS = 256
HALF = 768
QUART = HALF // 2
WIDE = 2 * HALF + 128
GATE = (slice(0, QUART), slice(WIDE - 2 * QUART, WIDE - QUART))
UP = (slice(QUART, 2 * QUART), slice(WIDE - QUART, WIDE))
SQ = slice(2 * QUART, 2 * QUART + 128)
PIECE = (slice(0, 2 * QUART + 128), slice(2 * QUART + 128, WIDE))
NEG = -1e30
EPS = 1e-6
CENTERS = (-6, -3, 0, 3, 6)
FAR = (6, -6, 3, -3)
PLANE = sorted(
    ((dy, dx) for dy in range(4) for dx in range(4) if dy or dx), key=lambda s: -sum(min(v, 4 - v) for v in s)
)


def remote(src, dst, send, recv, dev):
    return pltpu.make_async_remote_copy(
        src_ref=src, dst_ref=dst, send_sem=send, recv_sem=recv, device_id=dev, device_id_type=MESH
    )


def dot(a, b):
    return jnp.dot(a, b, preferred_element_type=F32)


def dot_t(a, b):
    return lax.dot_general(a, b, (((0,), (0,)), ((), ())), preferred_element_type=F32)


def dot_nt(a, b):
    return lax.dot_general(a, b, (((1,), (1,)), ((), ())), preferred_element_type=F32)


def hi_lo(v, rows):
    high = v.astype(BF).astype(F32)
    lane = lax.broadcasted_iota(jnp.int32, (rows, 128), 1)
    return jnp.where(lane < 64, high, v - high).astype(BF)


def split3(v):
    high = v.astype(BF).astype(F32)
    mid = (v - high).astype(BF).astype(F32)
    return [high, mid, v - high - mid]


def from_hi_lo(block):
    return jnp.sum(block, axis=1, keepdims=True) * (1.0 / 64.0)


def kernel(
    len_hbm, q_hbm, nk_hbm, nv_hbm, kc_ref, vc_ref, op_ref, res_ref, gain_hbm, gw_ref, uw_ref, dw_ref,
    ids_hbm, rw_hbm, o_ref,
    len_ref, q_ref, nk_ref, nv_ref, gain_ref, ids_ref, rw_ref,
    kc, vc, opw, resb, gainb, wg, wu, wd, resf,
    acc, acc_in, wt, attn, cs1, cr1, cs2, cr2,
    nb, hid, sel_in, sel_out, slot_w, part, from_left, from_right, from_far, s2, r2, act, mo, fr,
    loc, snd, rcv, bulk_s, bulk_r, far_ready,
):
    r = lax.axis_index("req")
    e = lax.axis_index("exp")
    z = r // 2
    c = lax.rem(r, 2)
    oc = 1 - c
    ex = lax.rem(e, 4)
    ey = e // 4

    def at_z(off):
        return (2 * lax.rem(z + off + NZ, NZ) + c, e)

    sibling = (2 * z + oc, e)

    barrier = pltpu.get_barrier_semaphore()

    def greet(dev):
        pl.semaphore_signal(barrier, inc=1, device_id=dev, device_id_type=MESH)

    def plane(step):
        return lax.rem(ey + step[0], 4) * 4 + lax.rem(ex + step[1], 4)

    for step in PLANE:
        greet((r, plane(step)))
    for off in (3, -3, 2, -2, 1, -1):
        greet(at_z(off))
    greet(sibling)

    copies = []

    def fetch(src, dst):
        cp = pltpu.make_async_copy(src, dst, loc.at[len(copies)])
        cp.start()
        copies.append(cp)
        return cp

    cache_copies = [
        fetch(len_hbm, len_ref), fetch(q_hbm, q_ref), fetch(nk_hbm, nk_ref), fetch(nv_hbm, nv_ref),
    ]
    for s in range(2):
        cache_copies.append(fetch(kc_ref.at[s], kc.at[s]))
        cache_copies.append(fetch(vc_ref.at[s], vc.at[s]))
    mine = pl.multiple_of(c * HALF, 128)
    theirs = pl.multiple_of(oc * HALF, 128)
    early = [
        fetch(gain_hbm, gain_ref), fetch(ids_hbm, ids_ref), fetch(rw_hbm, rw_ref),
        fetch(op_ref, opw.at[c]), fetch(res_ref, resb.at[c]),
    ]
    weights = [
        fetch(gw_ref.at[:, :, pl.ds(mine, HALF)], wg.at[:, c]),
        fetch(uw_ref.at[:, :, pl.ds(mine, HALF)], wu.at[:, c]),
        fetch(dw_ref.at[:, pl.ds(mine, HALF), :], wd.at[:, c]),
    ]
    lane = lax.broadcasted_iota(jnp.int32, (1, 128), 1)
    lane_slot = lax.rem(lane, 8) // 4
    lane_step = lax.rem(lane, 4)
    first = lane_slot == 0
    for cp in cache_copies:
        cp.wait()
    n0 = len_ref[2 * r]
    n1 = len_ref[2 * r + 1]
    count = jnp.where(first, n0, n1)
    place = lax.broadcasted_iota(jnp.int32, (384, 128), 0) * NE + e
    live = place < count
    fresh_row = lax.broadcasted_iota(jnp.int32, (16, 128), 0)
    fresh_live = (
        (fresh_row < 8)
        & (fresh_row // 4 == lane_slot)
        & (lax.rem(fresh_row, 4) <= lane_step)
        & (jnp.zeros((16, 128), jnp.int32) + e == 0)
    )
    zeros8 = jnp.zeros((8, 512), F32)
    fresh_k = jnp.concatenate([nk_ref[...].astype(F32), zeros8], axis=0).astype(BF)
    fresh_v = jnp.concatenate([nv_ref[...].astype(F32), zeros8], axis=0).astype(BF)
    scale = HD ** (-0.5)
    for g in range(GROUPS):
        cols = slice(g * HD, (g + 1) * HD)
        q = jnp.concatenate(
            [q_ref[:, (g * 16 + j) * HD:(g * 16 + j + 1) * HD].astype(F32) for j in range(16)], axis=0
        ).astype(BF)
        s0 = dot_nt(kc[0, :, cols], q)
        s1 = dot_nt(kc[1, :, cols], q)
        score = jnp.where(live, jnp.where(first, s0, s1) * scale, NEG)
        fresh = jnp.where(fresh_live, dot_nt(fresh_k[:, cols], q) * scale, NEG)
        top = jnp.maximum(jnp.max(score, axis=0, keepdims=True), jnp.max(fresh, axis=0, keepdims=True))
        w = jnp.where(live, jnp.exp(score - top), 0.0)
        wf = jnp.where(fresh_live, jnp.exp(fresh - top), 0.0)
        total = jnp.sum(w, axis=0, keepdims=True) + jnp.sum(wf, axis=0, keepdims=True)
        w0 = jnp.where(first, w, 0.0).astype(BF)
        w1 = jnp.where(first, 0.0, w).astype(BF)
        mixed = dot_t(w0, vc[0, :, cols]) + dot_t(w1, vc[1, :, cols]) + dot_t(wf.astype(BF), fresh_v[:, cols])
        stats = jnp.concatenate(split3(top) + split3(total) + [jnp.zeros((10, 128), F32)], axis=0).astype(BF)
        mixed = mixed.astype(BF)
        for i in range(4):
            acc[4 * g + i, 0:32] = mixed[32 * i:32 * i + 32]
            acc[4 * g + i, 32:48] = stats

    for cp in early:
        cp.wait()
    gainb[c] = jnp.broadcast_to(gain_ref[...], (8, 128))
    pl.semaphore_wait(barrier, NE - 1 + 6 + 1)

    for step in PLANE:
        other = plane(step)
        remote(acc.at[other], acc_in.at[e], bulk_s.at[0], bulk_r.at[0], (r, other)).start()

    for off in (3, -3):
        pl.semaphore_signal(far_ready, inc=1, device_id=at_z(off), device_id_type=MESH)

    sends = []

    def send(src, dst, dev):
        cp = remote(src, dst, snd.at[len(sends)], rcv.at[len(sends)], dev)
        cp.start()
        sends.append(cp)
        return cp

    opw_cp = send(op_ref, opw.at[c], sibling)
    res_cp = send(res_ref, resb.at[c], sibling)
    gain_cp = send(gainb.at[c], gainb.at[c], sibling)
    wg_cp = send(gw_ref.at[:, :, pl.ds(theirs, HALF)], wg.at[:, c], sibling)
    wu_cp = send(uw_ref.at[:, :, pl.ds(theirs, HALF)], wu.at[:, c], sibling)
    wd_cp = send(dw_ref.at[:, pl.ds(theirs, HALF), :], wd.at[:, c], sibling)

    acc_in[e] = acc[e]

    ids = ids_ref[...]
    rw = rw_ref[...]
    col = lax.broadcasted_iota(jnp.int32, (256, 256), 1)
    row = lax.broadcasted_iota(jnp.int32, (256, 256), 0)
    upto = jnp.where(row <= col, 1.0, 0.0).astype(BF)
    real = (lax.rem(col, 128) // 8) * 16 + (col // 128) * 8 + lax.rem(col, 8)
    perm = jnp.where(row == real, 1.0, 0.0).astype(BF)
    row8 = lax.broadcasted_iota(jnp.int32, (8, 256), 0)
    hit0 = ids == 2 * e
    hit1 = ids == 2 * e + 1
    on0 = jnp.max(jnp.where(hit0, 1.0, 0.0), axis=0, keepdims=True)
    on1 = jnp.max(jnp.where(hit1, 1.0, 0.0), axis=0, keepdims=True)
    rw0 = jnp.sum(jnp.where(hit0, rw, 0.0), axis=0, keepdims=True)
    rw1 = jnp.sum(jnp.where(hit1, rw, 0.0), axis=0, keepdims=True)
    on = jnp.where(row8 == 0, on0, jnp.where(row8 == 1, on1, 0.0))
    rank = dot(on.astype(BF), upto)
    pos = jnp.where(on > 0.5, rank, 0.0)
    pos_perm = dot(pos.astype(BF), perm)
    slot_id = lax.broadcasted_iota(jnp.int32, (128, 256), 0).astype(F32) + 1.0
    chosen = []
    for k, weight in ((0, rw0), (1, rw1)):
        here = pl.ds(128 * k, 128)
        sel_in[here, :] = jnp.where(pos_perm[k:k + 1, :] == slot_id, 1.0, 0.0).astype(BF)
        pick = jnp.where(pos[k:k + 1, :] == slot_id, 1.0, 0.0)
        slot_w[here, :] = jnp.broadcast_to(jnp.sum(pick * weight, axis=1, keepdims=True), (128, 128))
        chosen.append(pick)
    sel_out[...] = jnp.transpose(jnp.concatenate(chosen, axis=0)).astype(BF)

    pltpu.make_async_copy(acc_in.at[pl.ds(0, NE - 1)], acc_in.at[pl.ds(0, NE - 1)], bulk_r.at[0]).wait()
    stats = acc_in[:, 32:48, :].astype(F32)
    tops = stats[:, 0] + stats[:, 1] + stats[:, 2]
    totals = stats[:, 3] + stats[:, 4] + stats[:, 5]
    rel = jnp.exp(tops - jnp.max(tops, axis=0, keepdims=True))
    rel = rel / jnp.sum(rel * totals, axis=0, keepdims=True)
    wt[...] = jnp.transpose(jnp.concatenate([rel, jnp.zeros((112, 128), F32)], axis=0))
    shares = wt[pl.ds(pl.multiple_of(32 * ex, 32), 32), :]
    merged = shares[:, 0:1] * acc_in[0, 0:32].astype(F32)
    for src in range(1, NE):
        merged = merged + shares[:, src:src + 1] * acc_in[src, 0:32].astype(F32)
    attn[z] = merged.astype(BF)

    way = 1 - 2 * c

    def near(i):
        return lax.rem(i + 2 * NZ, NZ)

    class Gather:
        def __init__(self, chunk):
            self.chunk = chunk
            self.first_leg = {off: self.pass_on(0, off) for off in FAR}
            self.last_leg = [self.pass_on(0, off) for off in (1, -1)]

        def pass_on(self, off, step):
            block = self.chunk(near(z - off))
            return send(block, block, at_z(step))

        def forward(self):
            for off in (3, -3, 6, -6):
                self.first_leg[off].wait_recv()
                self.last_leg += [self.pass_on(off, step) for step in (1, -1)]
            self.last_leg.append(self.pass_on(6 * way, 2 * way))

        def finish(self):
            for cp in self.last_leg:
                cp.wait_recv()

    def gather(chunks):
        parts = [Gather(chunk) for chunk in chunks]
        for p in parts:
            p.forward()
        for p in parts:
            p.finish()

    pl.semaphore_wait(far_ready, 2)
    gather([lambda i: attn.at[i]])

    opw_cp.wait_recv()
    res_cp.wait_recv()
    gain_cp.wait_recv()
    for k in range(2):
        blocks = resb[k].astype(F32).reshape(NZ, 2, 8, 128)
        for t in range(2):
            resf[t, k] = blocks[:, t].reshape(128, 128)
    heads = attn[...].astype(F32).reshape(NZ, 4, 8, 128)
    x = jnp.concatenate([heads[:, j].reshape(128, 128) for j in range(4)], axis=1).astype(BF)

    def row_peer(i, row=r):
        return (row, ey * 4 + lax.rem(ex + i, 4))

    def column_peer(i, row=r):
        return (row, lax.rem(ey + i, 4) * 4 + ex)

    first_sum = []
    proj = []
    for k, peer in ((0, row_peer), (1, column_peer)):
        proj.append(dot(x, opw[k]))
        cs1[k] = proj[k].astype(BF)
        first_sum.append([send(cs1.at[k], cr1.at[k, i - 1], peer(i)) for i in (2, 1, 3)])
    second_sum = []
    for k, peer in ((0, column_peer), (1, row_peer)):
        for cp in first_sum[k]:
            cp.wait_recv()
        for i in range(3):
            proj[k] = proj[k] + cr1[k, i].astype(F32)
        cs2[k] = proj[k].astype(BF)
        legs = [send(cs2.at[k], cr2.at[c, k, i], peer(i)) for i in (2, 1, 3)]
        second_sum.append(legs)
    square = jnp.zeros((128, 128), F32)
    mine_rows = pl.ds(pl.multiple_of(128 * c, 128), 128)
    for k in range(2):
        for cp in second_sum[k]:
            cp.wait_recv()
        h = proj[k] + resf[c, k]
        for i in range(1, 4):
            h = h + cr2[c, k, i].astype(F32)
        hid[c, k] = h
        square = square + h * h
        nb[mine_rows, 128 * k:128 * k + 128] = (h * gainb[k, 0:1, :]).astype(BF)
    nb[mine_rows, 256:384] = hi_lo(jnp.sum(square, axis=1, keepdims=True), 128)
    nb_cp = send(nb.at[mine_rows], nb.at[mine_rows], sibling)
    hid_cp = send(hid.at[c, oc], hid.at[c, oc], sibling)

    for cp in weights:
        cp.wait()
    wg_cp.wait_recv()
    wu_cp.wait_recv()
    nb_cp.wait_recv()
    rows_in = dot(sel_in[...], nb[...])
    part[:, SQ] = hi_lo(from_hi_lo(rows_in[:, 256:384]), SLOTS)
    rows_in = rows_in[:, :256].astype(BF)
    for h in range(2):
        units = slice(QUART * h, QUART * h + QUART)
        for k in range(2):
            here = slice(128 * k, 128 * k + 128)
            part[here, GATE[h]] = dot(rows_in[here], wg[k, :, :, units].reshape(256, QUART)).astype(BF)
            part[here, UP[h]] = dot(rows_in[here], wu[k, :, :, units].reshape(256, QUART)).astype(BF)

    def rows_of(i):
        return pl.ds(pl.multiple_of(16 * near(i), 16), 16)

    far_cp = [None] * 2
    left_cp = {}
    right_cp = {}

    def collect(h, k):
        left_cp[h, k] = send(part.at[rows_of(z + 1 - CENTERS[k]), PIECE[h]], from_left.at[k, :, PIECE[h]], at_z(1))
        right_cp[h, k] = send(part.at[rows_of(z - 1 - CENTERS[k]), PIECE[h]], from_right.at[k, :, PIECE[h]], at_z(-1))

    for h in range(2):
        far_cp[h] = send(part.at[rows_of(z + 8), PIECE[h]], from_far.at[:, PIECE[h]], at_z(-2 * way))
        for k in (0, 4):
            collect(h, k)
    for h in range(2):
        for k in (1, 3):
            collect(h, k)

    def collected(h, k):
        left_cp[h, k].wait_recv()
        right_cp[h, k].wait_recv()
        rows = rows_of(z - CENTERS[k])
        return (
            part[rows, PIECE[h]].astype(F32)
            + from_left[k, :, PIECE[h]].astype(F32)
            + from_right[k, :, PIECE[h]].astype(F32)
        )

    hops = {}

    def pass_on(h, k, s, off):
        if h == 0:
            s2[k, :, 0:2 * QUART] = s[:, 0:2 * QUART].astype(BF)
            s2[k, :, SQ] = hi_lo(from_hi_lo(s[:, SQ]), 16)
        else:
            s2[k, :, PIECE[h]] = s.astype(BF)
        hops[h, k] = send(s2.at[k, :, PIECE[h]], r2.at[k, :, PIECE[h]], at_z(off))

    for h in range(2):
        far_cp[h].wait_recv()
        for k, core, off in ((0, 1, 3), (4, 0, -3)):
            far = jnp.where(c == core, from_far[:, PIECE[h]].astype(F32), 0.0)
            pass_on(h, k, collected(h, k) + far, off)
    for h in range(2):
        collect(h, 2)
    for h in range(2):
        for k, before, off in ((1, 0, 3), (3, 4, -3)):
            s = collected(h, k)
            hops[h, before].wait_recv()
            pass_on(h, k, s + r2[before, :, PIECE[h]].astype(F32), off)
    gathers = []
    for h in range(2):
        s = collected(h, 2)
        for k in (1, 3):
            hops[h, k].wait_recv()
            s = s + r2[k, :, PIECE[h]].astype(F32)
        if h == 0:
            norm = lax.rsqrt(from_hi_lo(s[:, SQ]) * (1.0 / D) + EPS)
        gate = norm * s[:, 0:QUART]
        up = norm * s[:, QUART:2 * QUART]
        units = slice(QUART * h, QUART * h + QUART)
        act[rows_of(z), units] = (gate / (1.0 + jnp.exp(-gate)) * up).astype(BF)
        gathers.append(Gather(lambda i, units=units: act.at[rows_of(i), units]))
    for p in gathers:
        p.forward()
    for p in gathers:
        p.finish()

    wd_cp.wait_recv()
    for k in range(2):
        down = jnp.concatenate([dot(act[128 * x2:128 * x2 + 128, :], wd[x2, k]) for x2 in range(2)], axis=0)
        mo[k] = dot(sel_out[...], (down * slot_w[...]).astype(BF)).astype(BF)

    def rows_for(other):
        return pl.ds(pl.multiple_of(16 * other, 16), 16)

    def out_send(other, core):
        remote(
            mo.at[core, rows_for(other)], fr.at[2 * e + c], bulk_s.at[1], bulk_r.at[1], (2 * z + core, other)
        ).start()

    for step in PLANE:
        for core in (c, oc):
            out_send(plane(step), core)
    out_send(e, oc)
    fr[2 * e + c] = mo[c, rows_for(e)]
    first_rows = pl.ds(pl.multiple_of(8 * e, 8), 8)
    hid_cp.wait_recv()
    base = jnp.concatenate([hid[0, c, first_rows], hid[1, c, first_rows]], axis=0)
    pltpu.make_async_copy(fr.at[pl.ds(0, 2 * NE - 1)], fr.at[pl.ds(0, 2 * NE - 1)], bulk_r.at[1]).wait()
    o_ref[...] = (base + jnp.sum(fr[...].astype(F32), axis=0)).astype(BF)

    for cp in sends:
        cp.wait_send()
    pltpu.make_async_copy(acc_in.at[pl.ds(0, NE - 1)], acc_in.at[pl.ds(0, NE - 1)], bulk_s.at[0]).wait()
    pltpu.make_async_copy(fr.at[pl.ds(0, 2 * NE - 1)], fr.at[pl.ds(0, 2 * NE - 1)], bulk_s.at[1]).wait()


def layer(
    queries, new_keys, new_values, key_cache, value_cache, lengths, out_proj, residual, norm_gain,
    gate_weight, up_weight, down_weight, expert_ids, route_weights,
):
    vmem = pl.BlockSpec(memory_space=pltpu.VMEM)
    hbm = pl.BlockSpec(memory_space=pltpu.HBM)
    scratch = [
        ((8, 8192), BF), ((8, 512), BF), ((8, 512), BF), ((1, 128), F32), ((8, 256), jnp.int32), ((8, 256), F32),
        ((2, 384, 512), BF), ((2, 384, 512), BF), ((2, 512, 128), BF), ((2, 256, 128), BF), ((2, 8, 128), F32),
        ((2, 2, 128, HALF), BF), ((2, 2, 128, HALF), BF), ((2, 2, HALF, 128), BF), ((2, 2, 128, 128), F32),
        ((16, 48, 128), BF), ((16, 48, 128), BF), ((128, 128), F32),
        ((16, 32, 128), BF), ((2, 128, 128), BF), ((2, 3, 128, 128), BF), ((2, 128, 128), BF),
        ((2, 2, 4, 128, 128), BF), ((256, 384), BF), ((2, 2, 128, 128), F32), ((256, 256), BF), ((256, 256), BF), ((256, 128), F32),
        ((256, WIDE), BF), ((5, 16, WIDE), BF), ((5, 16, WIDE), BF), ((16, WIDE), BF),
        ((5, 16, WIDE), BF), ((5, 16, WIDE), BF), ((256, HALF), BF),
        ((2, 256, 128), BF), ((32, 16, 128), BF),
    ]
    sems = [16, 112, 112, 2, 2]
    return pl.pallas_call(
        kernel,
        name="layer",
        out_shape=jax.ShapeDtypeStruct((16, 128), BF),
        in_specs=[hbm] * 14,
        out_specs=vmem,
        scratch_shapes=[pltpu.SMEM((64,), jnp.int32)] + [pltpu.VMEM(s, t) for s, t in scratch] + [pltpu.SemaphoreType.DMA((n,)) for n in sems] + [pltpu.SemaphoreType.REGULAR],
        compiler_params=pltpu.CompilerParams(
            collective_id=0, has_side_effects=True, vmem_limit_bytes=64 * 1024 * 1024
        ),
    )(
        lengths, queries, new_keys, new_values, key_cache[:, :, 0, :], value_cache[:, :, 0, :], out_proj, residual,
        norm_gain.reshape(1, 128), gate_weight, up_weight, down_weight, expert_ids.T, route_weights.T,
    )


def solution(mesh):
    in_specs = (
        P("req", None), P("req", None), P("req", None), P("req", None, "exp", None), P("req", None, "exp", None),
        P(), P("exp", "req"), P(None, "req"), P("req"), P("exp", "req", None), P("exp", "req", None),
        P("exp", None, "req"), P(), P(),
    )
    return jax.shard_map(layer, mesh=mesh, in_specs=in_specs, out_specs=P("exp", "req"), check_vma=False)
```

```python
import functools

import jax
import jax.numpy as jnp
from jax import lax
from jax.experimental import pallas as pl
from jax.experimental.pallas import tpu as pltpu
from jax.sharding import PartitionSpec as P

MESH = pl.DeviceIdType.MESH
BF = jnp.bfloat16
F32 = jnp.float32

D = 4096
HD = 128
GROUPS = 4
NZ = 16
NE = 16
SLOTS = 256
TOKENS = 256
HALF = 768
QUART = HALF // 2
WIDE = 2 * HALF + 128
GATE = (slice(0, QUART), slice(WIDE - 2 * QUART, WIDE - QUART))
UP = (slice(QUART, 2 * QUART), slice(WIDE - QUART, WIDE))
SQ = slice(2 * QUART, 2 * QUART + 128)
PIECE = (slice(0, 2 * QUART + 128), slice(2 * QUART + 128, WIDE))
NEG = -1e30
EPS = 1e-6
CENTERS = (-6, -3, 0, 3, 6)
FAR = (6, -6, 3, -3)
COLUMN = (8, 7, -7, 6, -6, 5, -5, 4, -4, 3, -3, 2, -2, 1, -1)
PLANE = sorted(
    ((dy, dx) for dy in range(4) for dx in range(4) if dy or dx), key=lambda s: -sum(min(v, 4 - v) for v in s)
)


def remote(src, dst, send, recv, dev):
    return pltpu.make_async_remote_copy(
        src_ref=src, dst_ref=dst, send_sem=send, recv_sem=recv, device_id=dev, device_id_type=MESH
    )


def dot(a, b):
    return jnp.dot(a, b, preferred_element_type=F32)


def dot_t(a, b):
    return lax.dot_general(a, b, (((0,), (0,)), ((), ())), preferred_element_type=F32)


def dot_nt(a, b):
    return lax.dot_general(a, b, (((1,), (1,)), ((), ())), preferred_element_type=F32)


def hi_lo(v, rows):
    high = v.astype(BF).astype(F32)
    lane = lax.broadcasted_iota(jnp.int32, (rows, 128), 1)
    return jnp.where(lane < 64, high, v - high).astype(BF)


def split3(v):
    high = v.astype(BF).astype(F32)
    mid = (v - high).astype(BF).astype(F32)
    return [high, mid, v - high - mid]


def from_hi_lo(block):
    return jnp.sum(block, axis=1, keepdims=True) * (1.0 / 64.0)


def kernel(
    len_hbm, q_hbm, nk_hbm, nv_hbm, kc_ref, vc_ref, op_ref, res_ref, gain_hbm, gw_ref, uw_ref, dw_ref,
    ids_hbm, rw_hbm, o_ref,
    len_ref, q_ref, nk_ref, nv_ref, gain_ref, ids_ref, rw_ref,
    kc, vc, opw, resb, gainb, wg, wu, wd, resf,
    acc, acc_in, wt, attn, cs1, cr1, cs2, cr2,
    nb, hid, sel_in, sel_out, slot_w, part, from_left, from_right, from_far, s2, r2, act, mo, fr,
    loc, snd, rcv, bulk_s, bulk_r, far_ready,
):
    r = lax.axis_index("req")
    e = lax.axis_index("exp")
    z = r // 2
    c = lax.rem(r, 2)
    oc = 1 - c
    ex = lax.rem(e, 4)
    ey = e // 4

    def at_z(off):
        return (2 * lax.rem(z + off + NZ, NZ) + c, e)

    sibling = (2 * z + oc, e)

    barrier = pltpu.get_barrier_semaphore()

    def greet(dev):
        pl.semaphore_signal(barrier, inc=1, device_id=dev, device_id_type=MESH)

    def plane(step):
        return lax.rem(ey + step[0], 4) * 4 + lax.rem(ex + step[1], 4)

    for step in PLANE:
        greet((r, plane(step)))
    for off in (4, -4, 3, -3, 2, -2, 1, -1):
        greet(at_z(off))
    greet(sibling)

    copies = []

    def fetch(src, dst):
        cp = pltpu.make_async_copy(src, dst, loc.at[len(copies)])
        cp.start()
        copies.append(cp)
        return cp

    cache_copies = [
        fetch(len_hbm, len_ref), fetch(q_hbm, q_ref), fetch(nk_hbm, nk_ref), fetch(nv_hbm, nv_ref),
    ]
    for s in range(2):
        cache_copies.append(fetch(kc_ref.at[s], kc.at[s]))
        cache_copies.append(fetch(vc_ref.at[s], vc.at[s]))
    mine = pl.multiple_of(c * HALF, 128)
    theirs = pl.multiple_of(oc * HALF, 128)
    early = [
        fetch(gain_hbm, gain_ref), fetch(ids_hbm, ids_ref), fetch(rw_hbm, rw_ref),
        fetch(op_ref, opw.at[c]), fetch(res_ref, resb.at[c]),
    ]
    weights = [
        fetch(gw_ref.at[:, :, pl.ds(mine, HALF)], wg.at[:, c]),
        fetch(uw_ref.at[:, :, pl.ds(mine, HALF)], wu.at[:, c]),
        fetch(dw_ref.at[:, pl.ds(mine, HALF), :], wd.at[:, c]),
    ]
    lane = lax.broadcasted_iota(jnp.int32, (1, 128), 1)
    lane_slot = lax.rem(lane, 8) // 4
    lane_step = lax.rem(lane, 4)
    first = lane_slot == 0
    for cp in cache_copies:
        cp.wait()
    n0 = len_ref[2 * r]
    n1 = len_ref[2 * r + 1]
    count = jnp.where(first, n0, n1)
    place = lax.broadcasted_iota(jnp.int32, (384, 128), 0) * NE + e
    live = place < count
    fresh_row = lax.broadcasted_iota(jnp.int32, (16, 128), 0)
    fresh_live = (
        (fresh_row < 8)
        & (fresh_row // 4 == lane_slot)
        & (lax.rem(fresh_row, 4) <= lane_step)
        & (jnp.zeros((16, 128), jnp.int32) + e == 0)
    )
    zeros8 = jnp.zeros((8, 512), F32)
    fresh_k = jnp.concatenate([nk_ref[...].astype(F32), zeros8], axis=0).astype(BF)
    fresh_v = jnp.concatenate([nv_ref[...].astype(F32), zeros8], axis=0).astype(BF)
    scale = HD ** (-0.5)
    for g in range(GROUPS):
        cols = slice(g * HD, (g + 1) * HD)
        q = jnp.concatenate(
            [q_ref[:, (g * 16 + j) * HD:(g * 16 + j + 1) * HD].astype(F32) for j in range(16)], axis=0
        ).astype(BF)
        s0 = dot_nt(kc[0, :, cols], q)
        s1 = dot_nt(kc[1, :, cols], q)
        score = jnp.where(live, jnp.where(first, s0, s1) * scale, NEG)
        fresh = jnp.where(fresh_live, dot_nt(fresh_k[:, cols], q) * scale, NEG)
        top = jnp.maximum(jnp.max(score, axis=0, keepdims=True), jnp.max(fresh, axis=0, keepdims=True))
        w = jnp.where(live, jnp.exp(score - top), 0.0)
        wf = jnp.where(fresh_live, jnp.exp(fresh - top), 0.0)
        total = jnp.sum(w, axis=0, keepdims=True) + jnp.sum(wf, axis=0, keepdims=True)
        w0 = jnp.where(first, w, 0.0).astype(BF)
        w1 = jnp.where(first, 0.0, w).astype(BF)
        mixed = dot_t(w0, vc[0, :, cols]) + dot_t(w1, vc[1, :, cols]) + dot_t(wf.astype(BF), fresh_v[:, cols])
        stats = jnp.concatenate(split3(top) + split3(total) + [jnp.zeros((10, 128), F32)], axis=0).astype(BF)
        mixed = mixed.astype(BF)
        for i in range(4):
            acc[4 * g + i, 0:32] = mixed[32 * i:32 * i + 32]
            acc[4 * g + i, 32:48] = stats

    for cp in early:
        cp.wait()
    gainb[c] = jnp.broadcast_to(gain_ref[...], (8, 128))
    pl.semaphore_wait(barrier, NE - 1 + 8 + 1)

    for step in PLANE:
        other = plane(step)
        remote(acc.at[other], acc_in.at[e], bulk_s.at[0], bulk_r.at[0], (r, other)).start()

    for off in (4, -4):
        pl.semaphore_signal(far_ready, inc=1, device_id=at_z(off), device_id_type=MESH)

    sends = []

    def send(src, dst, dev):
        cp = remote(src, dst, snd.at[len(sends)], rcv.at[len(sends)], dev)
        cp.start()
        sends.append(cp)
        return cp

    opw_cp = send(op_ref, opw.at[c], sibling)
    res_cp = send(res_ref, resb.at[c], sibling)
    gain_cp = send(gainb.at[c], gainb.at[c], sibling)
    wg_cp = send(gw_ref.at[:, :, pl.ds(theirs, HALF)], wg.at[:, c], sibling)
    wu_cp = send(uw_ref.at[:, :, pl.ds(theirs, HALF)], wu.at[:, c], sibling)
    wd_cp = send(dw_ref.at[:, pl.ds(theirs, HALF), :], wd.at[:, c], sibling)

    acc_in[e] = acc[e]

    ids = ids_ref[...]
    rw = rw_ref[...]
    col = lax.broadcasted_iota(jnp.int32, (256, 256), 1)
    row = lax.broadcasted_iota(jnp.int32, (256, 256), 0)
    upto = jnp.where(row <= col, 1.0, 0.0).astype(BF)
    real = (lax.rem(col, 128) // 8) * 16 + (col // 128) * 8 + lax.rem(col, 8)
    perm = jnp.where(row == real, 1.0, 0.0).astype(BF)
    row8 = lax.broadcasted_iota(jnp.int32, (8, 256), 0)
    hit0 = ids == 2 * e
    hit1 = ids == 2 * e + 1
    on0 = jnp.max(jnp.where(hit0, 1.0, 0.0), axis=0, keepdims=True)
    on1 = jnp.max(jnp.where(hit1, 1.0, 0.0), axis=0, keepdims=True)
    rw0 = jnp.sum(jnp.where(hit0, rw, 0.0), axis=0, keepdims=True)
    rw1 = jnp.sum(jnp.where(hit1, rw, 0.0), axis=0, keepdims=True)
    on = jnp.where(row8 == 0, on0, jnp.where(row8 == 1, on1, 0.0))
    rank = dot(on.astype(BF), upto)
    pos = jnp.where(on > 0.5, rank, 0.0)
    pos_perm = dot(pos.astype(BF), perm)
    slot_id = lax.broadcasted_iota(jnp.int32, (128, 256), 0).astype(F32) + 1.0
    chosen = []
    for k, weight in ((0, rw0), (1, rw1)):
        here = pl.ds(128 * k, 128)
        sel_in[here, :] = jnp.where(pos_perm[k:k + 1, :] == slot_id, 1.0, 0.0).astype(BF)
        pick = jnp.where(pos[k:k + 1, :] == slot_id, 1.0, 0.0)
        slot_w[here, :] = jnp.broadcast_to(jnp.sum(pick * weight, axis=1, keepdims=True), (128, 128))
        chosen.append(pick)
    sel_out[...] = jnp.transpose(jnp.concatenate(chosen, axis=0)).astype(BF)

    pltpu.make_async_copy(acc_in.at[pl.ds(0, NE - 1)], acc_in.at[pl.ds(0, NE - 1)], bulk_r.at[0]).wait()
    stats = acc_in[:, 32:48, :].astype(F32)
    tops = stats[:, 0] + stats[:, 1] + stats[:, 2]
    totals = stats[:, 3] + stats[:, 4] + stats[:, 5]
    rel = jnp.exp(tops - jnp.max(tops, axis=0, keepdims=True))
    rel = rel / jnp.sum(rel * totals, axis=0, keepdims=True)
    wt[...] = jnp.transpose(jnp.concatenate([rel, jnp.zeros((112, 128), F32)], axis=0))
    shares = wt[pl.ds(pl.multiple_of(32 * ex, 32), 32), :]
    merged = shares[:, 0:1] * acc_in[0, 0:32].astype(F32)
    for src in range(1, NE):
        merged = merged + shares[:, src:src + 1] * acc_in[src, 0:32].astype(F32)
    attn[z] = merged.astype(BF)

    way = 1 - 2 * c

    def near(i):
        return lax.rem(i + 2 * NZ, NZ)

    class Gather:
        def __init__(self, chunk):
            self.chunk = chunk
            self.first_leg = {off: self.pass_on(0, off) for off in FAR}
            self.last_leg = [self.pass_on(0, off) for off in (1, -1)]

        def pass_on(self, off, step):
            block = self.chunk(near(z - off))
            return send(block, block, at_z(step))

        def forward(self):
            for off in (3, -3, 6, -6):
                self.first_leg[off].wait_recv()
                self.last_leg += [self.pass_on(off, step) for step in (1, -1)]
            self.last_leg.append(self.pass_on(6 * way, 2 * way))

        def finish(self):
            for cp in self.last_leg:
                cp.wait_recv()

    pl.semaphore_wait(far_ready, 2)
    legs = [send(attn.at[z], attn.at[z], at_z(off)) for off in COLUMN]
    for cp in legs:
        cp.wait_recv()

    opw_cp.wait_recv()
    heads = attn[...].astype(F32).reshape(NZ, 4, 8, 128)
    x = jnp.concatenate([heads[:, j].reshape(128, 128) for j in range(4)], axis=1).astype(BF)

    def row_peer(i, row=r):
        return (row, ey * 4 + lax.rem(ex + i, 4))

    def column_peer(i, row=r):
        return (row, lax.rem(ey + i, 4) * 4 + ex)

    first_sum = []
    proj = []
    for k, peer in ((0, row_peer), (1, column_peer)):
        proj.append(dot(x, opw[k]))
        cs1[k] = proj[k].astype(BF)
        first_sum.append([send(cs1.at[k], cr1.at[k, i - 1], peer(i)) for i in (2, 1, 3)])
    res_cp.wait_recv()
    gain_cp.wait_recv()
    for k in range(2):
        blocks = resb[k].astype(F32).reshape(NZ, 2, 8, 128)
        for t in range(2):
            resf[t, k] = blocks[:, t].reshape(128, 128)
    second_sum = []
    for k, peer in ((0, column_peer), (1, row_peer)):
        for cp in first_sum[k]:
            cp.wait_recv()
        for i in range(3):
            proj[k] = proj[k] + cr1[k, i].astype(F32)
        cs2[k] = proj[k].astype(BF)
        legs = [send(cs2.at[k], cr2.at[c, k, i], peer(i)) for i in (2, 1, 3)]
        second_sum.append(legs)
    square = jnp.zeros((128, 128), F32)
    mine_rows = pl.ds(pl.multiple_of(128 * c, 128), 128)
    for k in range(2):
        for cp in second_sum[k]:
            cp.wait_recv()
        h = proj[k] + resf[c, k]
        for i in range(1, 4):
            h = h + cr2[c, k, i].astype(F32)
        hid[c, k] = h
        square = square + h * h
        nb[mine_rows, 128 * k:128 * k + 128] = (h * gainb[k, 0:1, :]).astype(BF)
    nb[mine_rows, 256:384] = hi_lo(jnp.sum(square, axis=1, keepdims=True), 128)
    nb_cp = send(nb.at[mine_rows], nb.at[mine_rows], sibling)

    for cp in weights:
        cp.wait()
    wg_cp.wait_recv()
    wu_cp.wait_recv()
    nb_cp.wait_recv()
    rows_in = dot(sel_in[...], nb[...])
    part[:, SQ] = hi_lo(from_hi_lo(rows_in[:, 256:384]), SLOTS)
    rows_in = rows_in[:, :256].astype(BF)
    def multiply(h):
        units = slice(QUART * h, QUART * h + QUART)
        for k in range(2):
            here = slice(128 * k, 128 * k + 128)
            part[here, GATE[h]] = dot(rows_in[here], wg[k, :, :, units].reshape(256, QUART)).astype(BF)
            part[here, UP[h]] = dot(rows_in[here], wu[k, :, :, units].reshape(256, QUART)).astype(BF)

    def rows_of(i):
        return pl.ds(pl.multiple_of(16 * near(i), 16), 16)

    far_cp = [None] * 2
    left_cp = {}
    right_cp = {}

    def collect(h, k):
        left_cp[h, k] = send(part.at[rows_of(z + 1 - CENTERS[k]), PIECE[h]], from_left.at[k, :, PIECE[h]], at_z(1))
        right_cp[h, k] = send(part.at[rows_of(z - 1 - CENTERS[k]), PIECE[h]], from_right.at[k, :, PIECE[h]], at_z(-1))

    for h in range(2):
        multiply(h)
        far_cp[h] = send(part.at[rows_of(z + 8), PIECE[h]], from_far.at[:, PIECE[h]], at_z(-2 * way))
        for k in (0, 4):
            collect(h, k)
    for h in range(2):
        for k in (1, 3):
            collect(h, k)
    hid_cp = send(hid.at[c, oc], hid.at[c, oc], sibling)

    def collected(h, k):
        left_cp[h, k].wait_recv()
        right_cp[h, k].wait_recv()
        rows = rows_of(z - CENTERS[k])
        return (
            part[rows, PIECE[h]].astype(F32)
            + from_left[k, :, PIECE[h]].astype(F32)
            + from_right[k, :, PIECE[h]].astype(F32)
        )

    hops = {}

    def pass_on(h, k, s, off):
        if h == 0:
            s2[k, :, 0:2 * QUART] = s[:, 0:2 * QUART].astype(BF)
            s2[k, :, SQ] = hi_lo(from_hi_lo(s[:, SQ]), 16)
        else:
            s2[k, :, PIECE[h]] = s.astype(BF)
        hops[h, k] = send(s2.at[k, :, PIECE[h]], r2.at[k, :, PIECE[h]], at_z(off))

    for h in range(2):
        far_cp[h].wait_recv()
        for k, core, off in ((0, 1, 3), (4, 0, -3)):
            far = jnp.where(c == core, from_far[:, PIECE[h]].astype(F32), 0.0)
            pass_on(h, k, collected(h, k) + far, off)
    for h in range(2):
        collect(h, 2)
    for h in range(2):
        for k, before, off in ((1, 0, 3), (3, 4, -3)):
            s = collected(h, k)
            hops[h, before].wait_recv()
            pass_on(h, k, s + r2[before, :, PIECE[h]].astype(F32), off)
    gathers = []
    for h in range(2):
        s = collected(h, 2)
        for k in (1, 3):
            hops[h, k].wait_recv()
            s = s + r2[k, :, PIECE[h]].astype(F32)
        if h == 0:
            norm = lax.rsqrt(from_hi_lo(s[:, SQ]) * (1.0 / D) + EPS)
        gate = norm * s[:, 0:QUART]
        up = norm * s[:, QUART:2 * QUART]
        units = slice(QUART * h, QUART * h + QUART)
        act[rows_of(z), units] = (gate / (1.0 + jnp.exp(-gate)) * up).astype(BF)
        gathers.append(Gather(lambda i, units=units: act.at[rows_of(i), units]))
    for p in gathers:
        p.forward()
    for p in gathers:
        p.finish()

    wd_cp.wait_recv()
    def rows_for(other):
        return pl.ds(pl.multiple_of(16 * other, 16), 16)

    def out_send(other, core):
        remote(
            mo.at[core, rows_for(other)], fr.at[2 * e + c], bulk_s.at[1], bulk_r.at[1], (2 * z + core, other)
        ).start()

    for k in range(2):
        down = jnp.concatenate([dot(act[128 * x2:128 * x2 + 128, :], wd[x2, k]) for x2 in range(2)], axis=0)
        mo[k] = dot(sel_out[...], (down * slot_w[...]).astype(BF)).astype(BF)
        for step in PLANE:
            out_send(plane(step), k)
    out_send(e, oc)
    fr[2 * e + c] = mo[c, rows_for(e)]
    for cp in sends:
        cp.wait_send()
    pltpu.make_async_copy(acc_in.at[pl.ds(0, NE - 1)], acc_in.at[pl.ds(0, NE - 1)], bulk_s.at[0]).wait()
    first_rows = pl.ds(pl.multiple_of(8 * e, 8), 8)
    hid_cp.wait_recv()
    base = jnp.concatenate([hid[0, c, first_rows], hid[1, c, first_rows]], axis=0)
    pltpu.make_async_copy(fr.at[pl.ds(0, 2 * NE - 1)], fr.at[pl.ds(0, 2 * NE - 1)], bulk_r.at[1]).wait()
    o_ref[...] = (base + jnp.sum(fr[...].astype(F32), axis=0)).astype(BF)

    pltpu.make_async_copy(fr.at[pl.ds(0, 2 * NE - 1)], fr.at[pl.ds(0, 2 * NE - 1)], bulk_s.at[1]).wait()


def layer(
    queries, new_keys, new_values, key_cache, value_cache, lengths, out_proj, residual, norm_gain,
    gate_weight, up_weight, down_weight, expert_ids, route_weights,
):
    vmem = pl.BlockSpec(memory_space=pltpu.VMEM)
    hbm = pl.BlockSpec(memory_space=pltpu.HBM)
    scratch = [
        ((8, 8192), BF), ((8, 512), BF), ((8, 512), BF), ((1, 128), F32), ((8, 256), jnp.int32), ((8, 256), F32),
        ((2, 384, 512), BF), ((2, 384, 512), BF), ((2, 512, 128), BF), ((2, 256, 128), BF), ((2, 8, 128), F32),
        ((2, 2, 128, HALF), BF), ((2, 2, 128, HALF), BF), ((2, 2, HALF, 128), BF), ((2, 2, 128, 128), F32),
        ((16, 48, 128), BF), ((16, 48, 128), BF), ((128, 128), F32),
        ((16, 32, 128), BF), ((2, 128, 128), BF), ((2, 3, 128, 128), BF), ((2, 128, 128), BF),
        ((2, 2, 4, 128, 128), BF), ((256, 384), BF), ((2, 2, 128, 128), F32), ((256, 256), BF), ((256, 256), BF), ((256, 128), F32),
        ((256, WIDE), BF), ((5, 16, WIDE), BF), ((5, 16, WIDE), BF), ((16, WIDE), BF),
        ((5, 16, WIDE), BF), ((5, 16, WIDE), BF), ((256, HALF), BF),
        ((2, 256, 128), BF), ((32, 16, 128), BF),
    ]
    sems = [16, 112, 112, 2, 2]
    return pl.pallas_call(
        kernel,
        name="layer",
        out_shape=jax.ShapeDtypeStruct((16, 128), BF),
        in_specs=[hbm] * 14,
        out_specs=vmem,
        scratch_shapes=[pltpu.SMEM((64,), jnp.int32)] + [pltpu.VMEM(s, t) for s, t in scratch] + [pltpu.SemaphoreType.DMA((n,)) for n in sems] + [pltpu.SemaphoreType.REGULAR],
        compiler_params=pltpu.CompilerParams(
            collective_id=0, has_side_effects=True, vmem_limit_bytes=64 * 1024 * 1024
        ),
    )(
        lengths, queries, new_keys, new_values, key_cache[:, :, 0, :], value_cache[:, :, 0, :], out_proj, residual,
        norm_gain.reshape(1, 128), gate_weight, up_weight, down_weight, expert_ids.T, route_weights.T,
    )


def solution(mesh):
    in_specs = (
        P("req", None), P("req", None), P("req", None), P("req", None, "exp", None), P("req", None, "exp", None),
        P(), P("exp", "req"), P(None, "req"), P("req"), P("exp", "req", None), P("exp", "req", None),
        P("exp", None, "req"), P(), P(),
    )
    return jax.shard_map(layer, mesh=mesh, in_specs=in_specs, out_specs=P("exp", "req"), check_vma=False)
```

```python
import functools

import jax
import jax.numpy as jnp
from jax import lax
from jax.experimental import pallas as pl
from jax.experimental.pallas import tpu as pltpu
from jax.sharding import PartitionSpec as P

MESH = pl.DeviceIdType.MESH
BF = jnp.bfloat16
F32 = jnp.float32

D = 4096
HD = 128
GROUPS = 4
NZ = 16
NE = 16
SLOTS = 256
TOKENS = 256
HALF = 768
QUART = HALF // 2
WIDE = 2 * HALF
GATE = (slice(0, QUART), slice(2 * QUART, 3 * QUART))
UP = (slice(QUART, 2 * QUART), slice(3 * QUART, WIDE))
PIECE = (slice(0, 2 * QUART), slice(2 * QUART, WIDE))
NEG = -1e30
EPS = 1e-6
CENTERS = (-6, -3, 0, 3, 6)
FAR = (6, -6, 3, -3)
COLUMN = (8, 7, -7, 6, -6, 5, -5, 4, -4, 3, -3, 2, -2, 1, -1)
PLANE = sorted(
    ((dy, dx) for dy in range(4) for dx in range(4) if dy or dx), key=lambda s: -sum(min(v, 4 - v) for v in s)
)


def remote(src, dst, send, recv, dev):
    return pltpu.make_async_remote_copy(
        src_ref=src, dst_ref=dst, send_sem=send, recv_sem=recv, device_id=dev, device_id_type=MESH
    )


def dot(a, b):
    return jnp.dot(a, b, preferred_element_type=F32)


def dot_t(a, b):
    return lax.dot_general(a, b, (((0,), (0,)), ((), ())), preferred_element_type=F32)


def dot_nt(a, b):
    return lax.dot_general(a, b, (((1,), (1,)), ((), ())), preferred_element_type=F32)


def split3(v):
    high = v.astype(BF).astype(F32)
    mid = (v - high).astype(BF).astype(F32)
    return [high, mid, v - high - mid]


def kernel(
    len_hbm, q_hbm, nk_hbm, nv_hbm, kc_ref, vc_ref, op_ref, res_ref, gain_hbm, gw_ref, uw_ref, dw_ref,
    ids_hbm, rw_hbm, o_ref,
    len_ref, q_ref, nk_ref, nv_ref, gain_ref, ids_ref, rw_ref,
    kc, vc, opw, resb, gainb, wg, wu, wd, resf,
    acc, acc_in, wt, attn, cs1, cr1, cs2, cr2,
    nb, hid, sq_in, sq, sel_in, sel_out, slot_w, part, from_left, from_right, from_far, s2, r2, act, mo, fr,
    loc, snd, rcv, bulk_s, bulk_r, far_ready,
):
    r = lax.axis_index("req")
    e = lax.axis_index("exp")
    z = r // 2
    c = lax.rem(r, 2)
    oc = 1 - c
    ex = lax.rem(e, 4)
    ey = e // 4

    def at_z(off):
        return (2 * lax.rem(z + off + NZ, NZ) + c, e)

    sibling = (2 * z + oc, e)

    barrier = pltpu.get_barrier_semaphore()

    def greet(dev):
        pl.semaphore_signal(barrier, inc=1, device_id=dev, device_id_type=MESH)

    def plane(step):
        return lax.rem(ey + step[0], 4) * 4 + lax.rem(ex + step[1], 4)

    for step in PLANE:
        greet((r, plane(step)))
    for off in (4, -4, 3, -3, 2, -2, 1, -1):
        greet(at_z(off))
    greet(sibling)

    copies = []

    def fetch(src, dst):
        cp = pltpu.make_async_copy(src, dst, loc.at[len(copies)])
        cp.start()
        copies.append(cp)
        return cp

    cache_copies = [
        fetch(len_hbm, len_ref), fetch(q_hbm, q_ref), fetch(nk_hbm, nk_ref), fetch(nv_hbm, nv_ref),
    ]
    for s in range(2):
        cache_copies.append(fetch(kc_ref.at[s], kc.at[s]))
        cache_copies.append(fetch(vc_ref.at[s], vc.at[s]))
    mine = pl.multiple_of(c * HALF, 128)
    theirs = pl.multiple_of(oc * HALF, 128)
    early = [
        fetch(gain_hbm, gain_ref), fetch(ids_hbm, ids_ref), fetch(rw_hbm, rw_ref),
        fetch(op_ref, opw.at[c]), fetch(res_ref, resb.at[c]),
    ]
    weights = [
        fetch(gw_ref.at[:, :, pl.ds(mine, HALF)], wg.at[:, c]),
        fetch(uw_ref.at[:, :, pl.ds(mine, HALF)], wu.at[:, c]),
        fetch(dw_ref.at[:, pl.ds(mine, HALF), :], wd.at[:, c]),
    ]
    lane = lax.broadcasted_iota(jnp.int32, (1, 128), 1)
    lane_slot = lax.rem(lane, 8) // 4
    lane_step = lax.rem(lane, 4)
    first = lane_slot == 0
    for cp in cache_copies:
        cp.wait()
    n0 = len_ref[2 * r]
    n1 = len_ref[2 * r + 1]
    count = jnp.where(first, n0, n1)
    place = lax.broadcasted_iota(jnp.int32, (384, 128), 0) * NE + e
    live = place < count
    fresh_row = lax.broadcasted_iota(jnp.int32, (16, 128), 0)
    fresh_live = (
        (fresh_row < 8)
        & (fresh_row // 4 == lane_slot)
        & (lax.rem(fresh_row, 4) <= lane_step)
        & (jnp.zeros((16, 128), jnp.int32) + e == 0)
    )
    zeros8 = jnp.zeros((8, 512), F32)
    fresh_k = jnp.concatenate([nk_ref[...].astype(F32), zeros8], axis=0).astype(BF)
    fresh_v = jnp.concatenate([nv_ref[...].astype(F32), zeros8], axis=0).astype(BF)
    scale = HD ** (-0.5)
    for g in range(GROUPS):
        cols = slice(g * HD, (g + 1) * HD)
        q = jnp.concatenate(
            [q_ref[:, (g * 16 + j) * HD:(g * 16 + j + 1) * HD].astype(F32) for j in range(16)], axis=0
        ).astype(BF)
        s0 = dot_nt(kc[0, :, cols], q)
        s1 = dot_nt(kc[1, :, cols], q)
        score = jnp.where(live, jnp.where(first, s0, s1) * scale, NEG)
        fresh = jnp.where(fresh_live, dot_nt(fresh_k[:, cols], q) * scale, NEG)
        top = jnp.maximum(jnp.max(score, axis=0, keepdims=True), jnp.max(fresh, axis=0, keepdims=True))
        w = jnp.where(live, jnp.exp(score - top), 0.0)
        wf = jnp.where(fresh_live, jnp.exp(fresh - top), 0.0)
        total = jnp.sum(w, axis=0, keepdims=True) + jnp.sum(wf, axis=0, keepdims=True)
        w0 = jnp.where(first, w, 0.0).astype(BF)
        w1 = jnp.where(first, 0.0, w).astype(BF)
        mixed = dot_t(w0, vc[0, :, cols]) + dot_t(w1, vc[1, :, cols]) + dot_t(wf.astype(BF), fresh_v[:, cols])
        stats = jnp.concatenate(split3(top) + split3(total) + [jnp.zeros((10, 128), F32)], axis=0).astype(BF)
        mixed = mixed.astype(BF)
        for i in range(4):
            acc[4 * g + i, 0:32] = mixed[32 * i:32 * i + 32]
            acc[4 * g + i, 32:48] = stats

    for cp in early:
        cp.wait()
    gainb[c] = jnp.broadcast_to(gain_ref[...], (8, 128))
    pl.semaphore_wait(barrier, NE - 1 + 8 + 1)

    for step in PLANE:
        other = plane(step)
        remote(acc.at[other], acc_in.at[e], bulk_s.at[0], bulk_r.at[0], (r, other)).start()

    for off in (4, -4):
        pl.semaphore_signal(far_ready, inc=1, device_id=at_z(off), device_id_type=MESH)

    sends = []

    def send(src, dst, dev):
        cp = remote(src, dst, snd.at[len(sends)], rcv.at[len(sends)], dev)
        cp.start()
        sends.append(cp)
        return cp

    opw_cp = send(op_ref, opw.at[c], sibling)
    res_cp = send(res_ref, resb.at[c], sibling)
    gain_cp = send(gainb.at[c], gainb.at[c], sibling)
    wg_cp = send(gw_ref.at[:, :, pl.ds(theirs, HALF)], wg.at[:, c], sibling)
    wu_cp = send(uw_ref.at[:, :, pl.ds(theirs, HALF)], wu.at[:, c], sibling)
    wd_cp = send(dw_ref.at[:, pl.ds(theirs, HALF), :], wd.at[:, c], sibling)

    acc_in[e] = acc[e]

    ids = ids_ref[...]
    rw = rw_ref[...]
    col = lax.broadcasted_iota(jnp.int32, (256, 256), 1)
    row = lax.broadcasted_iota(jnp.int32, (256, 256), 0)
    upto = jnp.where(row <= col, 1.0, 0.0).astype(BF)
    real = (lax.rem(col, 128) // 8) * 16 + (col // 128) * 8 + lax.rem(col, 8)
    perm = jnp.where(row == real, 1.0, 0.0).astype(BF)
    row8 = lax.broadcasted_iota(jnp.int32, (8, 256), 0)
    hit0 = ids == 2 * e
    hit1 = ids == 2 * e + 1
    on0 = jnp.max(jnp.where(hit0, 1.0, 0.0), axis=0, keepdims=True)
    on1 = jnp.max(jnp.where(hit1, 1.0, 0.0), axis=0, keepdims=True)
    rw0 = jnp.sum(jnp.where(hit0, rw, 0.0), axis=0, keepdims=True)
    rw1 = jnp.sum(jnp.where(hit1, rw, 0.0), axis=0, keepdims=True)
    on = jnp.where(row8 == 0, on0, jnp.where(row8 == 1, on1, 0.0))
    rank = dot(on.astype(BF), upto)
    pos = jnp.where(on > 0.5, rank, 0.0)
    pos_perm = dot(pos.astype(BF), perm)
    slot_id = lax.broadcasted_iota(jnp.int32, (128, 256), 0).astype(F32) + 1.0
    chosen = []
    for k, weight in ((0, rw0), (1, rw1)):
        here = pl.ds(128 * k, 128)
        sel_in[here, :] = jnp.where(pos_perm[k:k + 1, :] == slot_id, 1.0, 0.0).astype(BF)
        pick = jnp.where(pos[k:k + 1, :] == slot_id, 1.0, 0.0)
        slot_w[here, :] = jnp.broadcast_to(jnp.sum(pick * weight, axis=1, keepdims=True), (128, 128))
        chosen.append(pick)
    sel_out[...] = jnp.transpose(jnp.concatenate(chosen, axis=0)).astype(BF)

    pltpu.make_async_copy(acc_in.at[pl.ds(0, NE - 1)], acc_in.at[pl.ds(0, NE - 1)], bulk_r.at[0]).wait()
    stats = acc_in[:, 32:48, :].astype(F32)
    tops = stats[:, 0] + stats[:, 1] + stats[:, 2]
    totals = stats[:, 3] + stats[:, 4] + stats[:, 5]
    rel = jnp.exp(tops - jnp.max(tops, axis=0, keepdims=True))
    rel = rel / jnp.sum(rel * totals, axis=0, keepdims=True)
    wt[...] = jnp.transpose(jnp.concatenate([rel, jnp.zeros((112, 128), F32)], axis=0))
    shares = wt[pl.ds(pl.multiple_of(32 * ex, 32), 32), :]
    merged = shares[:, 0:1] * acc_in[0, 0:32].astype(F32)
    for src in range(1, NE):
        merged = merged + shares[:, src:src + 1] * acc_in[src, 0:32].astype(F32)
    attn[z] = merged.astype(BF)

    way = 1 - 2 * c

    def near(i):
        return lax.rem(i + 2 * NZ, NZ)

    class Gather:
        def __init__(self, chunk):
            self.chunk = chunk
            self.first_leg = {off: self.pass_on(0, off) for off in FAR}
            self.last_leg = [self.pass_on(0, off) for off in (1, -1)]

        def pass_on(self, off, step):
            block = self.chunk(near(z - off))
            return send(block, block, at_z(step))

        def forward(self):
            for off in (3, -3, 6, -6):
                self.first_leg[off].wait_recv()
                self.last_leg += [self.pass_on(off, step) for step in (1, -1)]
            self.last_leg.append(self.pass_on(6 * way, 2 * way))

        def finish(self):
            for cp in self.last_leg:
                cp.wait_recv()

    pl.semaphore_wait(far_ready, 2)
    legs = [send(attn.at[z], attn.at[z], at_z(off)) for off in COLUMN]
    for cp in legs:
        cp.wait_recv()

    opw_cp.wait_recv()
    heads = attn[...].astype(F32).reshape(NZ, 4, 8, 128)
    x = jnp.concatenate([heads[:, j].reshape(128, 128) for j in range(4)], axis=1).astype(BF)

    def row_peer(i, row=r):
        return (row, ey * 4 + lax.rem(ex + i, 4))

    def column_peer(i, row=r):
        return (row, lax.rem(ey + i, 4) * 4 + ex)

    first_sum = []
    proj = []
    for k, peer in ((0, row_peer), (1, column_peer)):
        proj.append(dot(x, opw[k]))
        cs1[k] = proj[k].astype(BF)
        first_sum.append([send(cs1.at[k], cr1.at[k, i - 1], peer(i)) for i in (2, 1, 3)])
    res_cp.wait_recv()
    gain_cp.wait_recv()
    for k in range(2):
        blocks = resb[k].astype(F32).reshape(NZ, 2, 8, 128)
        for t in range(2):
            resf[t, k] = blocks[:, t].reshape(128, 128)
    second_sum = []
    for k, peer in ((0, column_peer), (1, row_peer)):
        for cp in first_sum[k]:
            cp.wait_recv()
        for i in range(3):
            proj[k] = proj[k] + cr1[k, i].astype(F32)
        cs2[k] = proj[k].astype(BF)
        legs = [send(cs2.at[k], cr2.at[c, k, i], peer(i)) for i in (2, 1, 3)]
        second_sum.append(legs)
    square = jnp.zeros((128, 128), F32)
    mine_rows = pl.ds(pl.multiple_of(128 * c, 128), 128)
    for k in range(2):
        for cp in second_sum[k]:
            cp.wait_recv()
        h = proj[k] + resf[c, k]
        for i in range(1, 4):
            h = h + cr2[c, k, i].astype(F32)
        hid[c, k] = h
        square = square + h * h
        nb[mine_rows, 128 * k:128 * k + 128] = (h * gainb[k, 0:1, :]).astype(BF)
    nb_cp = send(nb.at[mine_rows], nb.at[mine_rows], sibling)
    sq_in[z] = jnp.sum(jnp.transpose(square), axis=0, keepdims=True)
    for off in COLUMN:
        remote(sq_in.at[z], sq_in.at[z], bulk_s.at[2], bulk_r.at[2], at_z(off)).start()

    for cp in weights:
        cp.wait()
    wg_cp.wait_recv()
    wu_cp.wait_recv()
    nb_cp.wait_recv()
    rows_in = dot(sel_in[...], nb[...]).astype(BF)
    def multiply(h):
        units = slice(QUART * h, QUART * h + QUART)
        for k in range(2):
            here = slice(128 * k, 128 * k + 128)
            part[here, GATE[h]] = dot(rows_in[here], wg[k, :, :, units].reshape(256, QUART)).astype(BF)
            part[here, UP[h]] = dot(rows_in[here], wu[k, :, :, units].reshape(256, QUART)).astype(BF)

    def rows_of(i):
        return pl.ds(pl.multiple_of(16 * near(i), 16), 16)

    far_cp = [None] * 2
    left_cp = {}
    right_cp = {}

    def collect(h, k):
        left_cp[h, k] = send(part.at[rows_of(z + 1 - CENTERS[k]), PIECE[h]], from_left.at[k, :, PIECE[h]], at_z(1))
        right_cp[h, k] = send(part.at[rows_of(z - 1 - CENTERS[k]), PIECE[h]], from_right.at[k, :, PIECE[h]], at_z(-1))

    for h in range(2):
        multiply(h)
        far_cp[h] = send(part.at[rows_of(z + 8), PIECE[h]], from_far.at[:, PIECE[h]], at_z(-2 * way))
        for k in (0, 4):
            collect(h, k)
    for h in range(2):
        for k in (1, 3):
            collect(h, k)
    hid_cp = send(hid.at[c, oc], hid.at[c, oc], sibling)

    def collected(h, k):
        left_cp[h, k].wait_recv()
        right_cp[h, k].wait_recv()
        rows = rows_of(z - CENTERS[k])
        return (
            part[rows, PIECE[h]].astype(F32)
            + from_left[k, :, PIECE[h]].astype(F32)
            + from_right[k, :, PIECE[h]].astype(F32)
        )

    hops = {}

    def pass_on(h, k, s, off):
        s2[k, :, PIECE[h]] = s.astype(BF)
        hops[h, k] = send(s2.at[k, :, PIECE[h]], r2.at[k, :, PIECE[h]], at_z(off))

    for h in range(2):
        far_cp[h].wait_recv()
        for k, core, off in ((0, 1, 3), (4, 0, -3)):
            far = jnp.where(c == core, from_far[:, PIECE[h]].astype(F32), 0.0)
            pass_on(h, k, collected(h, k) + far, off)
    for h in range(2):
        collect(h, 2)
    for h in range(2):
        for k, before, off in ((1, 0, 3), (3, 4, -3)):
            s = collected(h, k)
            hops[h, before].wait_recv()
            pass_on(h, k, s + r2[before, :, PIECE[h]].astype(F32), off)
    pltpu.make_async_copy(sq_in.at[pl.ds(0, NZ - 1)], sq_in.at[pl.ds(0, NZ - 1)], bulk_r.at[2]).wait()
    sq[c] = jnp.sum(sq_in[...], axis=0)
    sq_cp = send(sq.at[c], sq.at[c], sibling)
    sq_cp.wait_recv()
    owned = sel_in[rows_of(z), :].astype(F32)
    squares = jnp.sum(owned[:, :128] * sq[0] + owned[:, 128:] * sq[1], axis=1, keepdims=True)
    norm = lax.rsqrt(squares * (1.0 / D) + EPS)
    gathers = []
    for h in range(2):
        s = collected(h, 2)
        for k in (1, 3):
            hops[h, k].wait_recv()
            s = s + r2[k, :, PIECE[h]].astype(F32)
        gate = norm * s[:, 0:QUART]
        up = norm * s[:, QUART:2 * QUART]
        units = slice(QUART * h, QUART * h + QUART)
        act[rows_of(z), units] = (gate / (1.0 + jnp.exp(-gate)) * up).astype(BF)
        gathers.append(Gather(lambda i, units=units: act.at[rows_of(i), units]))
    for p in gathers:
        p.forward()
    for p in gathers:
        p.finish()

    wd_cp.wait_recv()
    def rows_for(other):
        return pl.ds(pl.multiple_of(16 * other, 16), 16)

    def out_send(other, core):
        remote(
            mo.at[core, rows_for(other)], fr.at[2 * e + c], bulk_s.at[1], bulk_r.at[1], (2 * z + core, other)
        ).start()

    for k in range(2):
        down = jnp.concatenate([dot(act[128 * x2:128 * x2 + 128, :], wd[x2, k]) for x2 in range(2)], axis=0)
        mo[k] = dot(sel_out[...], (down * slot_w[...]).astype(BF)).astype(BF)
        for step in PLANE:
            out_send(plane(step), k)
    out_send(e, oc)
    fr[2 * e + c] = mo[c, rows_for(e)]
    for cp in sends:
        cp.wait_send()
    pltpu.make_async_copy(acc_in.at[pl.ds(0, NE - 1)], acc_in.at[pl.ds(0, NE - 1)], bulk_s.at[0]).wait()
    pltpu.make_async_copy(sq_in.at[pl.ds(0, NZ - 1)], sq_in.at[pl.ds(0, NZ - 1)], bulk_s.at[2]).wait()
    first_rows = pl.ds(pl.multiple_of(8 * e, 8), 8)
    hid_cp.wait_recv()
    base = jnp.concatenate([hid[0, c, first_rows], hid[1, c, first_rows]], axis=0)
    pltpu.make_async_copy(fr.at[pl.ds(0, 2 * NE - 1)], fr.at[pl.ds(0, 2 * NE - 1)], bulk_r.at[1]).wait()
    o_ref[...] = (base + jnp.sum(fr[...].astype(F32), axis=0)).astype(BF)

    pltpu.make_async_copy(fr.at[pl.ds(0, 2 * NE - 1)], fr.at[pl.ds(0, 2 * NE - 1)], bulk_s.at[1]).wait()


def layer(
    queries, new_keys, new_values, key_cache, value_cache, lengths, out_proj, residual, norm_gain,
    gate_weight, up_weight, down_weight, expert_ids, route_weights,
):
    vmem = pl.BlockSpec(memory_space=pltpu.VMEM)
    hbm = pl.BlockSpec(memory_space=pltpu.HBM)
    scratch = [
        ((8, 8192), BF), ((8, 512), BF), ((8, 512), BF), ((1, 128), F32), ((8, 256), jnp.int32), ((8, 256), F32),
        ((2, 384, 512), BF), ((2, 384, 512), BF), ((2, 512, 128), BF), ((2, 256, 128), BF), ((2, 8, 128), F32),
        ((2, 2, 128, HALF), BF), ((2, 2, 128, HALF), BF), ((2, 2, HALF, 128), BF), ((2, 2, 128, 128), F32),
        ((16, 48, 128), BF), ((16, 48, 128), BF), ((128, 128), F32),
        ((16, 32, 128), BF), ((2, 128, 128), BF), ((2, 3, 128, 128), BF), ((2, 128, 128), BF),
        ((2, 2, 4, 128, 128), BF), ((256, 256), BF), ((2, 2, 128, 128), F32), ((16, 1, 128), F32), ((2, 1, 128), F32), ((256, 256), BF), ((256, 256), BF), ((256, 128), F32),
        ((256, WIDE), BF), ((5, 16, WIDE), BF), ((5, 16, WIDE), BF), ((16, WIDE), BF),
        ((5, 16, WIDE), BF), ((5, 16, WIDE), BF), ((256, HALF), BF),
        ((2, 256, 128), BF), ((32, 16, 128), BF),
    ]
    sems = [16, 112, 112, 3, 3]
    return pl.pallas_call(
        kernel,
        name="layer",
        out_shape=jax.ShapeDtypeStruct((16, 128), BF),
        in_specs=[hbm] * 14,
        out_specs=vmem,
        scratch_shapes=[pltpu.SMEM((64,), jnp.int32)] + [pltpu.VMEM(s, t) for s, t in scratch] + [pltpu.SemaphoreType.DMA((n,)) for n in sems] + [pltpu.SemaphoreType.REGULAR],
        compiler_params=pltpu.CompilerParams(
            collective_id=0, has_side_effects=True, vmem_limit_bytes=64 * 1024 * 1024
        ),
    )(
        lengths, queries, new_keys, new_values, key_cache[:, :, 0, :], value_cache[:, :, 0, :], out_proj, residual,
        norm_gain.reshape(1, 128), gate_weight, up_weight, down_weight, expert_ids.T, route_weights.T,
    )


def solution(mesh):
    in_specs = (
        P("req", None), P("req", None), P("req", None), P("req", None, "exp", None), P("req", None, "exp", None),
        P(), P("exp", "req"), P(None, "req"), P("req"), P("exp", "req", None), P("exp", "req", None),
        P("exp", None, "req"), P(), P(),
    )
    return jax.shard_map(layer, mesh=mesh, in_specs=in_specs, out_specs=P("exp", "req"), check_vma=False)
```

```python
import functools

import jax
import jax.numpy as jnp
from jax import lax
from jax.experimental import pallas as pl
from jax.experimental.pallas import tpu as pltpu
from jax.sharding import PartitionSpec as P

MESH = pl.DeviceIdType.MESH
BF = jnp.bfloat16
F32 = jnp.float32

D = 4096
HD = 128
GROUPS = 4
NZ = 16
NE = 16
SLOTS = 256
TOKENS = 256
HALF = 768
QUART = HALF // 2
WIDE = 2 * HALF
GATE = (slice(0, QUART), slice(2 * QUART, 3 * QUART))
UP = (slice(QUART, 2 * QUART), slice(3 * QUART, WIDE))
PIECE = (slice(0, 2 * QUART), slice(2 * QUART, WIDE))
NEG = -1e30
EPS = 1e-6
CENTERS = (-6, -3, 0, 3, 6)
FAR = (6, -6, 3, -3)
COLUMN = (8, 7, -7, 6, -6, 5, -5, 4, -4, 3, -3, 2, -2, 1, -1)
PLANE = sorted(
    ((dy, dx) for dy in range(4) for dx in range(4) if dy or dx), key=lambda s: -sum(min(v, 4 - v) for v in s)
)


def remote(src, dst, send, recv, dev):
    return pltpu.make_async_remote_copy(
        src_ref=src, dst_ref=dst, send_sem=send, recv_sem=recv, device_id=dev, device_id_type=MESH
    )


def dot(a, b):
    return jnp.dot(a, b, preferred_element_type=F32)


def dot_t(a, b):
    return lax.dot_general(a, b, (((0,), (0,)), ((), ())), preferred_element_type=F32)


def dot_nt(a, b):
    return lax.dot_general(a, b, (((1,), (1,)), ((), ())), preferred_element_type=F32)


def split3(v):
    high = v.astype(BF).astype(F32)
    mid = (v - high).astype(BF).astype(F32)
    return [high, mid, v - high - mid]


def kernel(
    len_hbm, q_hbm, nk_hbm, nv_hbm, kc_ref, vc_ref, op_ref, res_ref, gain_hbm, gw_ref, uw_ref, dw_ref,
    ids_hbm, rw_hbm, o_ref,
    len_ref, q_ref, nk_ref, nv_ref, gain_ref, ids_ref, rw_ref,
    kc, vc, opw, resb, gainb, wg, wu, wd, resf,
    acc, acc_in, wt, attn, cs1, cr1, cs2, cr2,
    nb, hid, sq_in, sq, sel_in, sel_out, slot_w, part, from_left, from_right, from_far, s2, r2, act, mo, fr,
    loc, snd, rcv, bulk_s, bulk_r, far_ready,
):
    r = lax.axis_index("req")
    e = lax.axis_index("exp")
    z = r // 2
    c = lax.rem(r, 2)
    oc = 1 - c
    ex = lax.rem(e, 4)
    ey = e // 4

    def at_z(off):
        return (2 * lax.rem(z + off + NZ, NZ) + c, e)

    sibling = (2 * z + oc, e)

    barrier = pltpu.get_barrier_semaphore()

    def greet(dev):
        pl.semaphore_signal(barrier, inc=1, device_id=dev, device_id_type=MESH)

    def plane(step):
        return lax.rem(ey + step[0], 4) * 4 + lax.rem(ex + step[1], 4)

    for step in PLANE:
        greet((r, plane(step)))
    for off in (4, -4, 3, -3, 2, -2, 1, -1):
        greet(at_z(off))
    greet(sibling)

    copies = []

    def fetch(src, dst):
        cp = pltpu.make_async_copy(src, dst, loc.at[len(copies)])
        cp.start()
        copies.append(cp)
        return cp

    cache_copies = [
        fetch(len_hbm, len_ref), fetch(q_hbm, q_ref), fetch(nk_hbm, nk_ref), fetch(nv_hbm, nv_ref),
    ]
    for s in range(2):
        cache_copies.append(fetch(kc_ref.at[s], kc.at[s]))
        cache_copies.append(fetch(vc_ref.at[s], vc.at[s]))
    mine = pl.multiple_of(c * HALF, 128)
    theirs = pl.multiple_of(oc * HALF, 128)
    early = [
        fetch(gain_hbm, gain_ref), fetch(ids_hbm, ids_ref), fetch(rw_hbm, rw_ref),
        fetch(op_ref, opw.at[c]), fetch(res_ref, resb.at[c]),
    ]
    weights = [
        fetch(gw_ref.at[:, :, pl.ds(mine, HALF)], wg.at[:, c]),
        fetch(uw_ref.at[:, :, pl.ds(mine, HALF)], wu.at[:, c]),
        fetch(dw_ref.at[:, pl.ds(mine, HALF), :], wd.at[:, c]),
    ]
    lane = lax.broadcasted_iota(jnp.int32, (1, 128), 1)
    lane_slot = lax.rem(lane, 8) // 4
    lane_step = lax.rem(lane, 4)
    first = lane_slot == 0
    for cp in cache_copies:
        cp.wait()
    n0 = len_ref[2 * r]
    n1 = len_ref[2 * r + 1]
    count = jnp.where(first, n0, n1)
    place = lax.broadcasted_iota(jnp.int32, (384, 128), 0) * NE + e
    live = place < count
    fresh_row = lax.broadcasted_iota(jnp.int32, (16, 128), 0)
    fresh_live = (
        (fresh_row < 8)
        & (fresh_row // 4 == lane_slot)
        & (lax.rem(fresh_row, 4) <= lane_step)
        & (jnp.zeros((16, 128), jnp.int32) + e == 0)
    )
    zeros8 = jnp.zeros((8, 512), F32)
    fresh_k = jnp.concatenate([nk_ref[...].astype(F32), zeros8], axis=0).astype(BF)
    fresh_v = jnp.concatenate([nv_ref[...].astype(F32), zeros8], axis=0).astype(BF)
    scale = HD ** (-0.5)
    for g in range(GROUPS):
        cols = slice(g * HD, (g + 1) * HD)
        q = jnp.concatenate(
            [q_ref[:, (g * 16 + j) * HD:(g * 16 + j + 1) * HD].astype(F32) for j in range(16)], axis=0
        ).astype(BF)
        s0 = dot_nt(kc[0, :, cols], q)
        s1 = dot_nt(kc[1, :, cols], q)
        score = jnp.where(live, jnp.where(first, s0, s1) * scale, NEG)
        fresh = jnp.where(fresh_live, dot_nt(fresh_k[:, cols], q) * scale, NEG)
        top = jnp.maximum(jnp.max(score, axis=0, keepdims=True), jnp.max(fresh, axis=0, keepdims=True))
        w = jnp.where(live, jnp.exp(score - top), 0.0)
        wf = jnp.where(fresh_live, jnp.exp(fresh - top), 0.0)
        total = jnp.sum(w, axis=0, keepdims=True) + jnp.sum(wf, axis=0, keepdims=True)
        w0 = jnp.where(first, w, 0.0).astype(BF)
        w1 = jnp.where(first, 0.0, w).astype(BF)
        mixed = dot_t(w0, vc[0, :, cols]) + dot_t(w1, vc[1, :, cols]) + dot_t(wf.astype(BF), fresh_v[:, cols])
        stats = jnp.concatenate(split3(top) + split3(total) + [jnp.zeros((10, 128), F32)], axis=0).astype(BF)
        mixed = mixed.astype(BF)
        for i in range(4):
            acc[4 * g + i, 0:32] = mixed[32 * i:32 * i + 32]
            acc[4 * g + i, 32:48] = stats

    for cp in early:
        cp.wait()
    gainb[c] = jnp.broadcast_to(gain_ref[...], (8, 128))
    pl.semaphore_wait(barrier, NE - 1 + 8 + 1)

    for step in PLANE:
        other = plane(step)
        remote(acc.at[other], acc_in.at[e], bulk_s.at[0], bulk_r.at[0], (r, other)).start()

    for off in (4, -4):
        pl.semaphore_signal(far_ready, inc=1, device_id=at_z(off), device_id_type=MESH)

    sends = []

    def send(src, dst, dev):
        cp = remote(src, dst, snd.at[len(sends)], rcv.at[len(sends)], dev)
        cp.start()
        sends.append(cp)
        return cp

    opw_cp = send(op_ref, opw.at[c], sibling)
    res_cp = send(res_ref, resb.at[c], sibling)
    gain_cp = send(gainb.at[c], gainb.at[c], sibling)
    wg_cp = send(gw_ref.at[:, :, pl.ds(theirs, HALF)], wg.at[:, c], sibling)
    wu_cp = send(uw_ref.at[:, :, pl.ds(theirs, HALF)], wu.at[:, c], sibling)
    wd_cp = send(dw_ref.at[:, pl.ds(theirs, HALF), :], wd.at[:, c], sibling)

    acc_in[e] = acc[e]

    ids = ids_ref[...]
    rw = rw_ref[...]
    col = lax.broadcasted_iota(jnp.int32, (256, 256), 1)
    row = lax.broadcasted_iota(jnp.int32, (256, 256), 0)
    upto = jnp.where(row <= col, 1.0, 0.0).astype(BF)
    real = (lax.rem(col, 128) // 8) * 16 + (col // 128) * 8 + lax.rem(col, 8)
    perm = jnp.where(row == real, 1.0, 0.0).astype(BF)
    row8 = lax.broadcasted_iota(jnp.int32, (8, 256), 0)
    hit0 = ids == 2 * e
    hit1 = ids == 2 * e + 1
    on0 = jnp.max(jnp.where(hit0, 1.0, 0.0), axis=0, keepdims=True)
    on1 = jnp.max(jnp.where(hit1, 1.0, 0.0), axis=0, keepdims=True)
    rw0 = jnp.sum(jnp.where(hit0, rw, 0.0), axis=0, keepdims=True)
    rw1 = jnp.sum(jnp.where(hit1, rw, 0.0), axis=0, keepdims=True)
    on = jnp.where(row8 == 0, on0, jnp.where(row8 == 1, on1, 0.0))
    rank = dot(on.astype(BF), upto)
    pos = jnp.where(on > 0.5, rank, 0.0)
    pos_perm = dot(pos.astype(BF), perm)
    slot_id = lax.broadcasted_iota(jnp.int32, (128, 256), 0).astype(F32) + 1.0
    chosen = []
    for k, weight in ((0, rw0), (1, rw1)):
        here = pl.ds(128 * k, 128)
        sel_in[here, :] = jnp.where(pos_perm[k:k + 1, :] == slot_id, 1.0, 0.0).astype(BF)
        pick = jnp.where(pos[k:k + 1, :] == slot_id, 1.0, 0.0)
        slot_w[here, :] = jnp.broadcast_to(jnp.sum(pick * weight, axis=1, keepdims=True), (128, 128))
        chosen.append(pick)
    sel_out[...] = jnp.transpose(jnp.concatenate(chosen, axis=0)).astype(BF)

    pltpu.make_async_copy(acc_in.at[pl.ds(0, NE - 1)], acc_in.at[pl.ds(0, NE - 1)], bulk_r.at[0]).wait()
    stats = acc_in[:, 32:48, :].astype(F32)
    tops = stats[:, 0] + stats[:, 1] + stats[:, 2]
    totals = stats[:, 3] + stats[:, 4] + stats[:, 5]
    rel = jnp.exp(tops - jnp.max(tops, axis=0, keepdims=True))
    rel = rel / jnp.sum(rel * totals, axis=0, keepdims=True)
    wt[...] = jnp.transpose(jnp.concatenate([rel, jnp.zeros((112, 128), F32)], axis=0))
    shares = wt[pl.ds(pl.multiple_of(32 * ex, 32), 32), :]
    merged = shares[:, 0:1] * acc_in[0, 0:32].astype(F32)
    for src in range(1, NE):
        merged = merged + shares[:, src:src + 1] * acc_in[src, 0:32].astype(F32)
    attn[z] = merged.astype(BF)

    way = 1 - 2 * c

    def near(i):
        return lax.rem(i + 2 * NZ, NZ)

    class Gather:
        def __init__(self, chunk):
            self.chunk = chunk
            self.first_leg = {off: self.pass_on(0, off) for off in FAR}
            self.last_leg = [self.pass_on(0, off) for off in (1, -1)]

        def pass_on(self, off, step):
            block = self.chunk(near(z - off))
            return send(block, block, at_z(step))

        def forward(self):
            for off in (3, -3, 6, -6):
                self.first_leg[off].wait_recv()
                self.last_leg += [self.pass_on(off, step) for step in (1, -1)]
            self.last_leg.append(self.pass_on(6 * way, 2 * way))

        def finish(self):
            for cp in self.last_leg:
                cp.wait_recv()

    pl.semaphore_wait(far_ready, 2)
    legs = [send(attn.at[z], attn.at[z], at_z(off)) for off in COLUMN]
    for cp in legs:
        cp.wait_recv()

    opw_cp.wait_recv()
    heads = attn[...].astype(F32).reshape(NZ, 4, 8, 128)
    x = jnp.concatenate([heads[:, j].reshape(128, 128) for j in range(4)], axis=1).astype(BF)

    def row_peer(i, row=r):
        return (row, ey * 4 + lax.rem(ex + i, 4))

    def column_peer(i, row=r):
        return (row, lax.rem(ey + i, 4) * 4 + ex)

    first_sum = []
    proj = []
    for k, peer in ((0, row_peer), (1, column_peer)):
        proj.append(dot(x, opw[k]))
        cs1[k] = proj[k].astype(BF)
        first_sum.append([send(cs1.at[k], cr1.at[k, i - 1], peer(i)) for i in (2, 1, 3)])
    res_cp.wait_recv()
    gain_cp.wait_recv()
    for k in range(2):
        blocks = resb[k].astype(F32).reshape(NZ, 2, 8, 128)
        for t in range(2):
            resf[t, k] = blocks[:, t].reshape(128, 128)
    second_sum = []
    for k, peer in ((0, column_peer), (1, row_peer)):
        for cp in first_sum[k]:
            cp.wait_recv()
        for i in range(3):
            proj[k] = proj[k] + cr1[k, i].astype(F32)
        cs2[k] = proj[k].astype(BF)
        legs = [send(cs2.at[k], cr2.at[c, k, i], peer(i)) for i in (2, 1, 3)]
        second_sum.append(legs)
    square = jnp.zeros((128, 128), F32)
    mine_rows = pl.ds(pl.multiple_of(128 * c, 128), 128)
    for k in range(2):
        for cp in second_sum[k]:
            cp.wait_recv()
        h = proj[k] + resf[c, k]
        for i in range(1, 4):
            h = h + cr2[c, k, i].astype(F32)
        hid[c, k] = h
        square = square + h * h
        nb[mine_rows, 128 * k:128 * k + 128] = (h * gainb[k, 0:1, :]).astype(BF)
    nb_cp = send(nb.at[mine_rows], nb.at[mine_rows], sibling)
    sq_in[z] = jnp.sum(jnp.transpose(square), axis=0, keepdims=True)
    for off in COLUMN:
        remote(sq_in.at[z], sq_in.at[z], bulk_s.at[2], bulk_r.at[2], at_z(off)).start()

    for cp in weights:
        cp.wait()
    wg_cp.wait_recv()
    wu_cp.wait_recv()
    nb_cp.wait_recv()
    rows_in = dot(sel_in[...], nb[...]).astype(BF)
    def multiply(h):
        units = slice(QUART * h, QUART * h + QUART)
        for k in range(2):
            here = slice(128 * k, 128 * k + 128)
            part[here, GATE[h]] = dot(rows_in[here], wg[k, :, :, units].reshape(256, QUART)).astype(BF)
            part[here, UP[h]] = dot(rows_in[here], wu[k, :, :, units].reshape(256, QUART)).astype(BF)

    def rows_of(i):
        return pl.ds(pl.multiple_of(16 * near(i), 16), 16)

    far_cp = [None] * 2
    left_cp = {}
    right_cp = {}

    def collect(h, k):
        left_cp[h, k] = send(part.at[rows_of(z + 1 - CENTERS[k]), PIECE[h]], from_left.at[k, :, PIECE[h]], at_z(1))
        right_cp[h, k] = send(part.at[rows_of(z - 1 - CENTERS[k]), PIECE[h]], from_right.at[k, :, PIECE[h]], at_z(-1))

    for h in range(2):
        multiply(h)
        far_cp[h] = send(part.at[rows_of(z + 8), PIECE[h]], from_far.at[:, PIECE[h]], at_z(-2 * way))
        for k in (0, 4):
            collect(h, k)
    for h in range(2):
        for k in (1, 3):
            collect(h, k)
    first_rows = pl.ds(pl.multiple_of(8 * e, 8), 8)
    hid_cp = send(hid.at[c, oc, first_rows], hid.at[c, oc, first_rows], sibling)

    def collected(h, k):
        left_cp[h, k].wait_recv()
        right_cp[h, k].wait_recv()
        rows = rows_of(z - CENTERS[k])
        return (
            part[rows, PIECE[h]].astype(F32)
            + from_left[k, :, PIECE[h]].astype(F32)
            + from_right[k, :, PIECE[h]].astype(F32)
        )

    hops = {}

    def pass_on(h, k, s, off):
        s2[k, :, PIECE[h]] = s.astype(BF)
        hops[h, k] = send(s2.at[k, :, PIECE[h]], r2.at[k, :, PIECE[h]], at_z(off))

    for h in range(2):
        far_cp[h].wait_recv()
        for k, core, off in ((0, 1, 3), (4, 0, -3)):
            far = jnp.where(c == core, from_far[:, PIECE[h]].astype(F32), 0.0)
            pass_on(h, k, collected(h, k) + far, off)
    for h in range(2):
        collect(h, 2)
    for h in range(2):
        for k, before, off in ((1, 0, 3), (3, 4, -3)):
            s = collected(h, k)
            hops[h, before].wait_recv()
            pass_on(h, k, s + r2[before, :, PIECE[h]].astype(F32), off)
    pltpu.make_async_copy(sq_in.at[pl.ds(0, NZ - 1)], sq_in.at[pl.ds(0, NZ - 1)], bulk_r.at[2]).wait()
    sq[c] = jnp.sum(sq_in[...], axis=0)
    sq_cp = send(sq.at[c], sq.at[c], sibling)
    sq_cp.wait_recv()
    owned = sel_in[rows_of(z), :].astype(F32)
    squares = jnp.sum(owned[:, :128] * sq[0] + owned[:, 128:] * sq[1], axis=1, keepdims=True)
    norm = lax.rsqrt(squares * (1.0 / D) + EPS)
    gathers = []
    for h in range(2):
        s = collected(h, 2)
        for k in (1, 3):
            hops[h, k].wait_recv()
            s = s + r2[k, :, PIECE[h]].astype(F32)
        gate = norm * s[:, 0:QUART]
        up = norm * s[:, QUART:2 * QUART]
        units = slice(QUART * h, QUART * h + QUART)
        act[rows_of(z), units] = (gate / (1.0 + jnp.exp(-gate)) * up).astype(BF)
        gathers.append(Gather(lambda i, units=units: act.at[rows_of(i), units]))
    for p in gathers:
        p.forward()
    wd_cp.wait_recv()
    down = [jnp.zeros((SLOTS, 128), F32)] * 2
    for h, p in enumerate(gathers):
        p.finish()
        units = slice(QUART * h, QUART * h + QUART)
        for k in range(2):
            both = [dot(act[128 * x2:128 * x2 + 128, units], wd[x2, k, units]) for x2 in range(2)]
            down[k] = down[k] + jnp.concatenate(both, axis=0)
    def rows_for(other):
        return pl.ds(pl.multiple_of(16 * other, 16), 16)

    def out_send(other, core):
        remote(
            mo.at[core, rows_for(other)], fr.at[2 * e + c], bulk_s.at[1], bulk_r.at[1], (2 * z + core, other)
        ).start()

    for k in range(2):
        mo[k] = dot(sel_out[...], (down[k] * slot_w[...]).astype(BF)).astype(BF)
        for step in PLANE:
            out_send(plane(step), k)
    out_send(e, oc)
    fr[2 * e + c] = mo[c, rows_for(e)]
    for cp in sends:
        cp.wait_send()
    pltpu.make_async_copy(acc_in.at[pl.ds(0, NE - 1)], acc_in.at[pl.ds(0, NE - 1)], bulk_s.at[0]).wait()
    pltpu.make_async_copy(sq_in.at[pl.ds(0, NZ - 1)], sq_in.at[pl.ds(0, NZ - 1)], bulk_s.at[2]).wait()
    hid_cp.wait_recv()
    base = jnp.concatenate([hid[0, c, first_rows], hid[1, c, first_rows]], axis=0)
    pltpu.make_async_copy(fr.at[pl.ds(0, 2 * NE - 1)], fr.at[pl.ds(0, 2 * NE - 1)], bulk_r.at[1]).wait()
    o_ref[...] = (base + jnp.sum(fr[...].astype(F32), axis=0)).astype(BF)

    pltpu.make_async_copy(fr.at[pl.ds(0, 2 * NE - 1)], fr.at[pl.ds(0, 2 * NE - 1)], bulk_s.at[1]).wait()


def layer(
    queries, new_keys, new_values, key_cache, value_cache, lengths, out_proj, residual, norm_gain,
    gate_weight, up_weight, down_weight, expert_ids, route_weights,
):
    vmem = pl.BlockSpec(memory_space=pltpu.VMEM)
    hbm = pl.BlockSpec(memory_space=pltpu.HBM)
    scratch = [
        ((8, 8192), BF), ((8, 512), BF), ((8, 512), BF), ((1, 128), F32), ((8, 256), jnp.int32), ((8, 256), F32),
        ((2, 384, 512), BF), ((2, 384, 512), BF), ((2, 512, 128), BF), ((2, 256, 128), BF), ((2, 8, 128), F32),
        ((2, 2, 128, HALF), BF), ((2, 2, 128, HALF), BF), ((2, 2, HALF, 128), BF), ((2, 2, 128, 128), F32),
        ((16, 48, 128), BF), ((16, 48, 128), BF), ((128, 128), F32),
        ((16, 32, 128), BF), ((2, 128, 128), BF), ((2, 3, 128, 128), BF), ((2, 128, 128), BF),
        ((2, 2, 4, 128, 128), BF), ((256, 256), BF), ((2, 2, 128, 128), F32), ((16, 1, 128), F32), ((2, 1, 128), F32), ((256, 256), BF), ((256, 256), BF), ((256, 128), F32),
        ((256, WIDE), BF), ((5, 16, WIDE), BF), ((5, 16, WIDE), BF), ((16, WIDE), BF),
        ((5, 16, WIDE), BF), ((5, 16, WIDE), BF), ((256, HALF), BF),
        ((2, 256, 128), BF), ((32, 16, 128), BF),
    ]
    sems = [16, 112, 112, 3, 3]
    return pl.pallas_call(
        kernel,
        name="layer",
        out_shape=jax.ShapeDtypeStruct((16, 128), BF),
        in_specs=[hbm] * 14,
        out_specs=vmem,
        scratch_shapes=[pltpu.SMEM((64,), jnp.int32)] + [pltpu.VMEM(s, t) for s, t in scratch] + [pltpu.SemaphoreType.DMA((n,)) for n in sems] + [pltpu.SemaphoreType.REGULAR],
        compiler_params=pltpu.CompilerParams(
            collective_id=0, has_side_effects=True, vmem_limit_bytes=64 * 1024 * 1024
        ),
    )(
        lengths, queries, new_keys, new_values, key_cache[:, :, 0, :], value_cache[:, :, 0, :], out_proj, residual,
        norm_gain.reshape(1, 128), gate_weight, up_weight, down_weight, expert_ids.T, route_weights.T,
    )


def solution(mesh):
    in_specs = (
        P("req", None), P("req", None), P("req", None), P("req", None, "exp", None), P("req", None, "exp", None),
        P(), P("exp", "req"), P(None, "req"), P("req"), P("exp", "req", None), P("exp", "req", None),
        P("exp", None, "req"), P(), P(),
    )
    return jax.shard_map(layer, mesh=mesh, in_specs=in_specs, out_specs=P("exp", "req"), check_vma=False)
```
